32 devices in a mesh: fibre: 8 (over z, x), seg: 4 (over y, core).
Axes of the slice: x: 2, y: 2, z: 4, core: 2. Of those that a mesh axis runs over, the one named last changes fastest.
Arguments:
- strain: float32 [768, 2048], P(('fibre', 'seg')), may hold values from -500 to 500
- fir_taps: float32 [64], replicated, may hold values from -0.75 to 0.75
- space_taps: float32 [31], replicated, may hold values from -1.2 to 1.2
- sources: int32 [3, 4], replicated, may hold values from 0 to 767, as said below
Outputs:
- correlations: float32 [3, 4, 768, 256], P(None, None, ('fibre', 'seg'))
The draws below stay inside these ranges and needn't reach their ends.
Inputs may be any that keep to these rules, and one draw needn't show every extreme that they name: `sources`: virtual-source channel indices; repeats are allowed.
All inputs are finite; a program needn't handle non-finite values.
Results may differ from the reference program's by a relative error of at most 0.0028.
Values may be sent and summed in bfloat16 or wider, within the bound.
No kernel may reach another device: no remote copies, remote signals or barrier semaphores. Data moves between devices by JAX's collectives and lax.ppermute only.
A program may use at most 64 MiB of HBM per device.

```python
import math
import jax
import jax.numpy as jnp
from jax import lax

CH_DEV = 24
SAMPLES = 2048
TAPS = 64
HALF = 15
RUN = 64
LAGS = 256
PANELS = 3
SRC = 4
CHANNELS = 768


def draw_strain(key, part):
    key_base, key_rows, key_blocks = jax.random.split(key, 3)
    base = jnp.clip(jax.random.normal(key_base, (CHANNELS, SAMPLES), jnp.float32), -6.0, 6.0)
    row_scale = jnp.exp(jax.random.uniform(key_rows, (CHANNELS, 1), jnp.float32, 0.0, math.log(10.0)))
    block_scale = jnp.exp(jax.random.uniform(key_blocks, (1, SAMPLES // 64), jnp.float32, 0.0, math.log(4.0)))
    column_scale = jnp.repeat(block_scale, 64, axis=1)
    return (base * row_scale * column_scale).astype(jnp.float32)


def draw_sources(key, part):
    key_centre, key_offset = jax.random.split(jax.random.fold_in(key, 7), 2)
    centres = jax.random.randint(key_centre, (PANELS, 1), 0, CHANNELS)
    offsets = jax.random.randint(key_offset, (PANELS, SRC), 0, 4 * CH_DEV)
    chosen = (centres + offsets) % CHANNELS
    chosen = chosen.at[0, 0].set(0)
    chosen = chosen.at[PANELS - 1, SRC - 1].set(CHANNELS - 1)
    return chosen.astype(jnp.int32)


def gaussian(key, extent, deviation, bound, dtype=jnp.bfloat16):
    values = deviation * jax.random.normal(key, extent, jnp.float32)
    return jnp.clip(values, min=-bound, max=bound).astype(dtype)


def setup_inputs(seed: int = 0) -> dict:
    seeds = jax.random.split(jax.random.key(seed), 5)
    strain = draw_strain(jax.random.fold_in(seeds[4], 71), 0)
    fir_taps = gaussian(seeds[1], (TAPS,), 0.125, 0.75, jnp.float32)
    space_taps = gaussian(seeds[2], (2 * HALF + 1,), 0.2, 1.2, jnp.float32)
    sources = draw_sources(jax.random.fold_in(seeds[4], 71), 0)
    return {"strain": strain, "fir_taps": fir_taps, "space_taps": space_taps, "sources": sources}


def reference(strain, fir_taps, space_taps, sources):
    channel_count = strain.shape[0]
    sample_count = strain.shape[1]
    padded = jnp.pad(strain, ((0, 0), (TAPS - 1, 0)))

    def fir_step(shift_index, accum):
        piece = lax.dynamic_slice_in_dim(padded, TAPS - 1 - shift_index, sample_count, 1)
        return accum + fir_taps[shift_index] * piece

    filtered = lax.fori_loop(0, TAPS, fir_step, jnp.zeros(strain.shape, jnp.float32))
    padded_rows = jnp.pad(filtered, ((HALF, HALF), (0, 0)))

    def space_step(shift_index, accum):
        piece = lax.dynamic_slice_in_dim(padded_rows, shift_index, channel_count, 0)
        return accum + space_taps[shift_index] * piece

    smoothed = lax.fori_loop(0, 2 * HALF + 1, space_step, jnp.zeros(strain.shape, jnp.float32))
    magnitude = jnp.pad(jnp.abs(smoothed), ((0, 0), (RUN, RUN)))

    def run_step(shift_index, accum):
        return accum + lax.dynamic_slice_in_dim(magnitude, shift_index, sample_count, 1)

    window_sum = lax.fori_loop(0, 2 * RUN + 1, run_step, jnp.zeros(strain.shape, jnp.float32))
    positions = jnp.arange(sample_count)
    window_count = (jnp.minimum(positions, RUN) + jnp.minimum(sample_count - 1 - positions, RUN) + 1).astype(jnp.float32)
    level = window_sum / window_count[None, :]
    normed = (smoothed / (level + 1e-5)).astype(jnp.bfloat16)
    length = sample_count + LAGS
    spectra = jnp.fft.rfft(normed.astype(jnp.float32), length, axis=1)
    flat_sources = sources.reshape(-1).astype(jnp.int32)
    norm_factor = float(sample_count) ** -0.5

    def correlate(channel):
        record = jnp.take(normed, channel, axis=0).astype(jnp.float32)
        source_spectrum = jnp.fft.rfft(record, length)
        circular = jnp.fft.irfft(jnp.conj(source_spectrum)[None, :] * spectra, length, axis=1)
        kept = jnp.concatenate([circular[:, length - LAGS // 2:], circular[:, :LAGS // 2]], axis=1)
        return (kept * norm_factor).astype(jnp.float32)

    result = lax.map(correlate, flat_sources)
    return result.reshape(PANELS, SRC, channel_count, LAGS)
```

```python
import functools

import jax
import jax.numpy as jnp
from jax import lax
from jax.experimental import pallas as pl
from jax.experimental.pallas import tpu as pltpu
from jax.sharding import PartitionSpec as P

RUN = 64
LAGS = 256
PANELS = 3
SRC = 4
AXES = ("fibre", "seg")
LANES = 128
STEP = 16
HALO = 16
ROWS = PANELS * SRC
HALF_ROWS = ROWS // 2
VMEM = pl.BlockSpec(memory_space=pltpu.VMEM)
SMEM = pl.BlockSpec(memory_space=pltpu.SMEM)
BF16 = jnp.bfloat16
F32 = jnp.float32


def split(x):
    high = x.astype(BF16)
    return high, (x - high.astype(F32)).astype(BF16)


def split_rows(x):
    high = x.astype(BF16).astype(F32)
    return jnp.concatenate([high, x - high, high], axis=0).astype(BF16)


def split_columns(x):
    high = x.astype(BF16).astype(F32)
    return jnp.concatenate([high, high, x - high], axis=1).astype(BF16)


def taps_at(taps_ref, index):
    total = jnp.zeros(index.shape, F32)
    for j in range(taps_ref.shape[0]):
        total = jnp.where(index == j, taps_ref[j], total)
    return total


def fir_matrix(fir_ref):
    lane = lax.broadcasted_iota(jnp.int32, (8, LANES), 1)
    row = lax.broadcasted_iota(jnp.int32, (8, LANES), 0)
    first = taps_at(fir_ref, lane - row)
    first = jnp.concatenate([first, jnp.zeros_like(first)], axis=1)
    return jnp.concatenate(
        [first if g == 0 else pltpu.roll(first, 8 * g, 1) for g in range(LANES // 8)], axis=0
    )


def to_blocks(x):
    return jnp.concatenate(
        [x[:, k : k + LANES] for k in range(0, x.shape[1], LANES)], axis=0
    )


def from_blocks(x, rows):
    return jnp.concatenate([x[k : k + rows] for k in range(0, x.shape[0], rows)], axis=1)


def earlier(x, rows):
    return jnp.concatenate([jnp.zeros((rows, x.shape[1]), x.dtype), x[:-rows]], axis=0)


def later(x, rows):
    return jnp.concatenate([x[rows:], jnp.zeros((rows, x.shape[1]), x.dtype)], axis=0)


def filter_and_norm(x, fir_both, fir_low):
    rows, samples = x.shape
    high, low = split(to_blocks(x))
    dot = functools.partial(jnp.dot, preferred_element_type=F32)
    full = dot(jnp.concatenate([high, low], axis=1), fir_both) + dot(high, fir_low)
    smooth = full[:, :LANES] + earlier(full[:, LANES:], rows)
    high, low = split(jnp.abs(smooth))
    u = lax.broadcasted_iota(jnp.int32, (2 * LANES, LANES), 0) % LANES
    t = lax.broadcasted_iota(jnp.int32, (2 * LANES, LANES), 1)
    bands = [jnp.abs(u - t) <= RUN, u - t >= LANES - RUN, t - u >= LANES - RUN]
    window = jnp.concatenate([jnp.where(b, 1.0, 0.0).astype(BF16) for b in bands], axis=1)
    sums = dot(jnp.concatenate([high, low], axis=1), window)
    total = (
        sums[:, :LANES]
        + earlier(sums[:, LANES : 2 * LANES], rows)
        + later(sums[:, 2 * LANES :], rows)
    )
    shape = total.shape
    where = lax.broadcasted_iota(jnp.int32, shape, 0) // rows * LANES
    where = where + lax.broadcasted_iota(jnp.int32, shape, 1)
    count = jnp.minimum(where, RUN) + jnp.minimum(samples - 1 - where, RUN) + 1
    level = total / count.astype(F32)
    return from_blocks(smooth / (level + 1e-5), rows)


def pack(x):
    width = x.shape[1] // 4
    tail = x[:, 3 * width :]
    more = [
        jnp.concatenate([tail[k : k + 1] for k in range(3 * g, 3 * g + 3)], axis=1)
        for g in range(2)
    ]
    return jnp.concatenate([x[:, : 3 * width]] + more, axis=0)


def unpack(x):
    width = x.shape[1] // 3
    tail = [x[6 + k // 3 : 7 + k // 3, k % 3 * width : (k % 3 + 1) * width] for k in range(6)]
    return jnp.concatenate([x[:6], jnp.concatenate(tail, axis=0)], axis=1)


def share_kernel(strain_ref, space_ref, sources_ref, keep_ref, send_ref, first_ref, last_ref):
    channels = strain_ref.shape[0]
    me = lax.axis_index(AXES)
    core = me % 2
    half_span = (space_ref.shape[0] - 1) // 2
    x = strain_ref[...]
    first_ref[...] = x[:HALO]
    last_ref[...] = x[channels - HALO :]
    row = lax.broadcasted_iota(jnp.int32, (16, channels), 0)
    lane = lax.broadcasted_iota(jnp.int32, (16, channels), 1)
    source = jnp.full((16, channels), -(1 << 20), jnp.int32)
    for k in range(ROWS):
        half = core if k < HALF_ROWS else 1 - core
        number = half * HALF_ROWS + k % HALF_ROWS
        place = k if k < HALF_ROWS else k - HALF_ROWS + 8
        source = jnp.where(row == place, sources_ref[number // SRC, number % SRC], source)
    matrix = taps_at(space_ref, lane + me * channels - source + half_span)
    share = jnp.dot(split_columns(matrix), split_rows(x), preferred_element_type=F32)
    keep_ref[...] = pack(share[:HALF_ROWS])
    send_ref[...] = pack(share[8 : 8 + HALF_ROWS])


def channels_kernel(
    strain_ref, before_ref, after_ref, fir_ref, space_ref, shifted_ref, both_ref, low_ref
):
    channels, samples = strain_ref.shape
    half_span = (space_ref.shape[0] - 1) // 2
    x = jnp.concatenate([before_ref[...], strain_ref[...], after_ref[...]], axis=0)
    wide = x.shape[0]
    row = lax.broadcasted_iota(jnp.int32, (channels, wide), 0)
    column = lax.broadcasted_iota(jnp.int32, (channels, wide), 1)
    matrix = taps_at(space_ref, column - HALO - row + half_span)
    spaced = jnp.dot(split_columns(matrix), split_rows(x), preferred_element_type=F32)
    high, low = split(fir_matrix(fir_ref))
    both = jnp.concatenate([high, high], axis=0)
    both_ref[...] = both
    low_ref[...] = low
    normed = filter_and_norm(spaced, both, low)
    length = shifted_ref.shape[1]
    padded = jnp.concatenate(
        [
            jnp.zeros((channels, LANES), F32),
            normed,
            jnp.zeros((channels, 2 * LANES), F32),
        ],
        axis=1,
    )
    per_tile = LANES // STEP
    for q in range(0, per_tile, 2):
        turned = [
            padded if k == 0 else pltpu.roll(padded, padded.shape[1] - STEP * k, 1)
            for k in (q, q + 1)
        ]
        pair = jnp.concatenate(turned, axis=0).astype(BF16)
        for h in range(LAGS // LANES):
            at = (h * per_tile + q) * channels
            shifted_ref[at : at + 2 * channels, :] = pair[:, h * LANES : h * LANES + length]


def swap(upper, lower, distance, lane):
    near = (lane // distance) % 2 == 0
    return (
        jnp.where(near, upper, pltpu.roll(lower, distance, 1)),
        jnp.where(near, pltpu.roll(upper, LANES - distance, 1), lower),
    )


def correlate_kernel(mine_ref, other_ref, shifted_ref, both_ref, low_ref, out_ref):
    channels = out_ref.shape[2]
    core = lax.axis_index(AXES) % 2
    mine = unpack(mine_ref[...])
    other = unpack(other_ref[...])
    samples = mine.shape[1]
    even = core == 0
    spaced = jnp.concatenate(
        [
            jnp.where(even, mine, other),
            jnp.where(even, other, mine),
            jnp.zeros((16 - ROWS, samples), F32),
        ],
        axis=0,
    )
    normed = filter_and_norm(spaced, both_ref[...], low_ref[...])
    normed = normed.astype(BF16).astype(F32)
    padded = jnp.concatenate([normed, jnp.zeros((16, LANES), F32)], axis=1)
    lane = lax.broadcasted_iota(jnp.int32, (STEP, LANES), 1)
    row = lax.broadcasted_iota(jnp.int32, (STEP, LANES), 0)
    straight = lane >= row
    records = []
    for k in range(ROWS):
        one = jnp.broadcast_to(padded[k : k + 1], (STEP, padded.shape[1]))
        tiles = [
            pltpu.roll(one[:, j : j + LANES], 0, 1, stride=1, stride_axis=0)
            for j in range(0, padded.shape[1], LANES)
        ]
        previous = [tiles[-1]] + tiles[:-1]
        records.append(
            jnp.concatenate(
                [jnp.where(straight, b, a) for a, b in zip(previous, tiles)], axis=1
            ).astype(BF16)
        )
    records = jnp.concatenate(records, axis=0)
    result = lax.dot_general(
        shifted_ref[...], records, (((1,), (1,)), ((), ())), preferred_element_type=F32
    )
    result = result * float(samples) ** -0.5
    result = jnp.concatenate(
        [result, jnp.zeros((result.shape[0], 2 * LANES - result.shape[1]), F32)], axis=1
    )
    per_tile = LANES // STEP
    lane = lax.broadcasted_iota(jnp.int32, (channels, LANES), 1)
    for h in range(LAGS // LANES):
        for tile in range(2):
            parts = [
                result[
                    (h * per_tile + q) * channels : (h * per_tile + q + 1) * channels,
                    tile * LANES : (tile + 1) * LANES,
                ]
                for q in range(per_tile)
            ]
            for distance in (4, 2, 1):
                for q in range(per_tile):
                    if q & distance == 0:
                        parts[q], parts[q + distance] = swap(
                            parts[q], parts[q + distance], distance * STEP, lane
                        )
            for q in range(per_tile):
                number = tile * per_tile + q
                if number < ROWS:
                    out_ref[number // SRC, number % SRC, :, h * LANES : (h + 1) * LANES] = parts[q]


def local(strain, fir_taps, space_taps, sources):
    channels, samples = strain.shape
    devices = lax.axis_size(AXES)
    packed = jax.ShapeDtypeStruct((8, samples * 3 // 4), F32)
    edge = jax.ShapeDtypeStruct((HALO, samples), F32)
    keep, send, first, last = pl.pallas_call(
        share_kernel,
        out_shape=[packed, packed, edge, edge],
        in_specs=[VMEM, SMEM, SMEM],
        out_specs=[VMEM] * 4,
        name="share",
    )(strain, space_taps, sources)

    def partner(x, distance):
        return lax.ppermute(x, AXES, [(i, i ^ distance) for i in range(devices)])

    total = keep + partner(send, 1)
    up = [(i, i + 1) for i in range(devices - 1)]
    before = lax.ppermute(last, AXES, up)
    after = lax.ppermute(first, AXES, [(j, i) for i, j in up])
    distance = 2
    while distance < devices:
        total = total + partner(total, distance)
        distance *= 2
    other = partner(total, 1)
    length = samples + LANES
    shifted, both, low = pl.pallas_call(
        channels_kernel,
        out_shape=[
            jax.ShapeDtypeStruct((LAGS // STEP * channels, length), BF16),
            jax.ShapeDtypeStruct((2 * LANES, 2 * LANES), BF16),
            jax.ShapeDtypeStruct((LANES, 2 * LANES), BF16),
        ],
        in_specs=[VMEM, VMEM, VMEM, SMEM, SMEM],
        out_specs=[VMEM] * 3,
        name="channels",
    )(strain, before, after, fir_taps, space_taps)
    return pl.pallas_call(
        correlate_kernel,
        out_shape=jax.ShapeDtypeStruct((PANELS, SRC, channels, LAGS), F32),
        in_specs=[VMEM] * 5,
        out_specs=VMEM,
        name="correlate",
    )(total, other, shifted, both, low)


def solution(mesh):
    return jax.shard_map(
        local,
        mesh=mesh,
        in_specs=(P(AXES, None), P(), P(), P()),
        out_specs=P(None, None, AXES, None),
        check_vma=False,
    )
```

```python
import functools

import jax
import jax.numpy as jnp
from jax import lax
from jax.experimental import pallas as pl
from jax.experimental.pallas import tpu as pltpu
from jax.sharding import PartitionSpec as P

RUN = 64
LAGS = 256
PANELS = 3
SRC = 4
AXES = ("fibre", "seg")
LANES = 128
STEP = 16
HALO = 16
ROWS = PANELS * SRC
HALF_ROWS = ROWS // 2
VMEM = pl.BlockSpec(memory_space=pltpu.VMEM)
HBM = pl.BlockSpec(memory_space=pltpu.HBM)
SMALL = pltpu.CompilerParams(vmem_limit_bytes=16 * 2**20)
BF16 = jnp.bfloat16
F32 = jnp.float32


def split(x):
    high = x.astype(BF16)
    return high, (x - high.astype(F32)).astype(BF16)


def split_rows(x):
    high = x.astype(BF16).astype(F32)
    return jnp.concatenate([high, x - high, high], axis=0).astype(BF16)


def split_columns(x):
    high = x.astype(BF16).astype(F32)
    return jnp.concatenate([high, high, x - high], axis=1).astype(BF16)


def taps_at(taps_ref, index):
    total = jnp.zeros(index.shape, F32)
    for j in range(taps_ref.shape[0]):
        total = jnp.where(index == j, taps_ref[j], total)
    return total


def fir_matrix(fir_ref):
    lane = lax.broadcasted_iota(jnp.int32, (8, LANES), 1)
    row = lax.broadcasted_iota(jnp.int32, (8, LANES), 0)
    first = taps_at(fir_ref, lane - row)
    first = jnp.concatenate([first, jnp.zeros_like(first)], axis=1)
    return jnp.concatenate(
        [first if g == 0 else pltpu.roll(first, 8 * g, 1) for g in range(LANES // 8)], axis=0
    )


def to_blocks(x):
    return jnp.concatenate(
        [x[:, k : k + LANES] for k in range(0, x.shape[1], LANES)], axis=0
    )


def from_blocks(x, rows):
    return jnp.concatenate([x[k : k + rows] for k in range(0, x.shape[0], rows)], axis=1)


def earlier(x, rows):
    return jnp.concatenate([jnp.zeros((rows, x.shape[1]), x.dtype), x[:-rows]], axis=0)


def later(x, rows):
    return jnp.concatenate([x[rows:], jnp.zeros((rows, x.shape[1]), x.dtype)], axis=0)


def filter_and_norm(x, fir_both, fir_low):
    rows, samples = x.shape
    high, low = split(to_blocks(x))
    dot = functools.partial(jnp.dot, preferred_element_type=F32)
    full = dot(jnp.concatenate([high, low], axis=1), fir_both) + dot(high, fir_low)
    smooth = full[:, :LANES] + earlier(full[:, LANES:], rows)
    high, low = split(jnp.abs(smooth))
    u = lax.broadcasted_iota(jnp.int32, (2 * LANES, LANES), 0) % LANES
    t = lax.broadcasted_iota(jnp.int32, (2 * LANES, LANES), 1)
    bands = [jnp.abs(u - t) <= RUN, u - t >= LANES - RUN, t - u >= LANES - RUN]
    window = jnp.concatenate([jnp.where(b, 1.0, 0.0).astype(BF16) for b in bands], axis=1)
    sums = dot(jnp.concatenate([high, low], axis=1), window)
    total = (
        sums[:, :LANES]
        + earlier(sums[:, LANES : 2 * LANES], rows)
        + later(sums[:, 2 * LANES :], rows)
    )
    shape = total.shape
    where = lax.broadcasted_iota(jnp.int32, shape, 0) // rows * LANES
    where = where + lax.broadcasted_iota(jnp.int32, shape, 1)
    count = jnp.minimum(where, RUN) + jnp.minimum(samples - 1 - where, RUN) + 1
    level = total / count.astype(F32)
    return from_blocks(smooth / (level + 1e-5), rows)


def pack(x):
    width = x.shape[1] // 4
    tail = x[:, 3 * width :]
    more = [
        jnp.concatenate([tail[k : k + 1] for k in range(3 * g, 3 * g + 3)], axis=1)
        for g in range(2)
    ]
    return jnp.concatenate([x[:, : 3 * width]] + more, axis=0)


def unpack(x):
    width = x.shape[1] // 3
    tail = [x[6 + k // 3 : 7 + k // 3, k % 3 * width : (k % 3 + 1) * width] for k in range(6)]
    return jnp.concatenate([x[:6], jnp.concatenate(tail, axis=0)], axis=1)


def fetch(pairs, sems):
    copies = [pltpu.make_async_copy(a, b, sems.at[i]) for i, (a, b) in enumerate(pairs)]
    for copy in copies:
        copy.start()
    return copies


def share_kernel(
    strain_hbm,
    space_hbm,
    sources_hbm,
    keep_ref,
    send_ref,
    inner_ref,
    outer_ref,
    strain_ref,
    space_ref,
    sources_ref,
    sems,
):
    copies = fetch(
        [(sources_hbm, sources_ref), (space_hbm, space_ref), (strain_hbm, strain_ref)], sems
    )
    channels = strain_ref.shape[0]
    me = lax.axis_index(AXES)
    core = me % 2
    half_span = (space_ref.shape[0] - 1) // 2
    even = core == 0
    copies[0].wait()
    row = lax.broadcasted_iota(jnp.int32, (16, channels), 0)
    lane = lax.broadcasted_iota(jnp.int32, (16, channels), 1)
    source = jnp.full((16, channels), -(1 << 20), jnp.int32)
    for k in range(ROWS):
        half = core if k < HALF_ROWS else 1 - core
        number = half * HALF_ROWS + k % HALF_ROWS
        place = k if k < HALF_ROWS else k - HALF_ROWS + 8
        source = jnp.where(row == place, sources_ref[number // SRC, number % SRC], source)
    copies[1].wait()
    matrix = taps_at(space_ref, lane + me * channels - source + half_span)
    copies[2].wait()
    x = strain_ref[...]
    inner_ref[...] = jnp.where(even, x[channels - HALO :], x[:HALO])
    outer_ref[...] = jnp.where(even, x[:HALO], x[channels - HALO :])
    share = jnp.dot(split_columns(matrix), split_rows(x), preferred_element_type=F32)
    keep_ref[...] = pack(share[:HALF_ROWS])
    send_ref[...] = pack(share[8 : 8 + HALF_ROWS])


def channels_kernel(
    strain_ref,
    inner_ref,
    outer_ref,
    fir_hbm,
    space_hbm,
    shifted_ref,
    both_ref,
    low_ref,
    fir_ref,
    space_ref,
    sems,
):
    copies = fetch([(space_hbm, space_ref), (fir_hbm, fir_ref)], sems)
    channels, samples = strain_ref.shape
    half_span = (space_ref.shape[0] - 1) // 2
    even = lax.axis_index(AXES) % 2 == 0
    inner, outer = inner_ref[...], outer_ref[...]
    before, after = jnp.where(even, outer, inner), jnp.where(even, inner, outer)
    x = jnp.concatenate([before, strain_ref[...], after], axis=0)
    wide = x.shape[0]
    row = lax.broadcasted_iota(jnp.int32, (channels, wide), 0)
    column = lax.broadcasted_iota(jnp.int32, (channels, wide), 1)
    copies[0].wait()
    matrix = taps_at(space_ref, column - HALO - row + half_span)
    spaced = jnp.dot(split_columns(matrix), split_rows(x), preferred_element_type=F32)
    copies[1].wait()
    high, low = split(fir_matrix(fir_ref))
    both = jnp.concatenate([high, high], axis=0)
    both_ref[...] = both
    low_ref[...] = low
    normed = filter_and_norm(spaced, both, low)
    length = shifted_ref.shape[1]
    padded = jnp.concatenate(
        [
            jnp.zeros((channels, LANES), F32),
            normed,
            jnp.zeros((channels, 2 * LANES), F32),
        ],
        axis=1,
    )
    per_tile = LANES // STEP
    for q in range(0, per_tile, 2):
        turned = [
            padded if k == 0 else pltpu.roll(padded, padded.shape[1] - STEP * k, 1)
            for k in (q, q + 1)
        ]
        pair = jnp.concatenate(turned, axis=0).astype(BF16)
        for h in range(LAGS // LANES):
            at = (h * per_tile + q) * channels
            shifted_ref[at : at + 2 * channels, :] = pair[:, h * LANES : h * LANES + length]


def swap(upper, lower, distance, lane):
    near = (lane // distance) % 2 == 0
    return (
        jnp.where(near, upper, pltpu.roll(lower, distance, 1)),
        jnp.where(near, pltpu.roll(upper, LANES - distance, 1), lower),
    )


def correlate_kernel(mine_ref, other_ref, shifted_ref, both_ref, low_ref, out_ref):
    channels = out_ref.shape[2]
    core = lax.axis_index(AXES) % 2
    mine = unpack(mine_ref[...])
    other = unpack(other_ref[...])
    samples = mine.shape[1]
    even = core == 0
    spaced = jnp.concatenate(
        [
            jnp.where(even, mine, other),
            jnp.where(even, other, mine),
            jnp.zeros((16 - ROWS, samples), F32),
        ],
        axis=0,
    )
    normed = filter_and_norm(spaced, both_ref[...], low_ref[...])
    normed = normed.astype(BF16).astype(F32)
    padded = jnp.concatenate([normed, jnp.zeros((16, LANES), F32)], axis=1)
    lane = lax.broadcasted_iota(jnp.int32, (STEP, LANES), 1)
    row = lax.broadcasted_iota(jnp.int32, (STEP, LANES), 0)
    straight = lane >= row
    records = []
    for k in range(ROWS):
        one = jnp.broadcast_to(padded[k : k + 1], (STEP, padded.shape[1]))
        tiles = [
            pltpu.roll(one[:, j : j + LANES], 0, 1, stride=1, stride_axis=0)
            for j in range(0, padded.shape[1], LANES)
        ]
        previous = [tiles[-1]] + tiles[:-1]
        records.append(
            jnp.concatenate(
                [jnp.where(straight, b, a) for a, b in zip(previous, tiles)], axis=1
            ).astype(BF16)
        )
    records = jnp.concatenate(records, axis=0)
    result = lax.dot_general(
        shifted_ref[...], records, (((1,), (1,)), ((), ())), preferred_element_type=F32
    )
    result = result * float(samples) ** -0.5
    result = jnp.concatenate(
        [result, jnp.zeros((result.shape[0], 2 * LANES - result.shape[1]), F32)], axis=1
    )
    per_tile = LANES // STEP
    lane = lax.broadcasted_iota(jnp.int32, (channels, LANES), 1)
    for h in range(LAGS // LANES):
        for tile in range(2):
            parts = [
                result[
                    (h * per_tile + q) * channels : (h * per_tile + q + 1) * channels,
                    tile * LANES : (tile + 1) * LANES,
                ]
                for q in range(per_tile)
            ]
            for distance in (4, 2, 1):
                for q in range(per_tile):
                    if q & distance == 0:
                        parts[q], parts[q + distance] = swap(
                            parts[q], parts[q + distance], distance * STEP, lane
                        )
            for q in range(per_tile):
                number = tile * per_tile + q
                if number < ROWS:
                    out_ref[number // SRC, number % SRC, :, h * LANES : (h + 1) * LANES] = parts[q]


def in_hbm(x):
    return pltpu.with_memory_space_constraint(x, pltpu.HBM)


def local(strain, fir_taps, space_taps, sources):
    channels, samples = strain.shape
    devices = lax.axis_size(AXES)
    packed = jax.ShapeDtypeStruct((8, samples * 3 // 4), F32)
    edge = jax.ShapeDtypeStruct((HALO, samples), F32)
    near = jax.ShapeDtypeStruct(strain.shape, F32)
    keep, send, inner, outer, near = pl.pallas_call(
        share_kernel,
        out_shape=[packed, packed, edge, edge, near],
        in_specs=[HBM] * 3,
        out_specs=[VMEM] * 5,
        scratch_shapes=[
            pltpu.SMEM(space_taps.shape, F32),
            pltpu.SMEM(sources.shape, jnp.int32),
            pltpu.SemaphoreType.DMA((3,)),
        ],
        compiler_params=SMALL,
        name="share",
    )(*[in_hbm(x) for x in (strain, space_taps, sources)])

    def partner(x, distance):
        return lax.ppermute(x, AXES, [(i, i ^ distance) for i in range(devices)])

    total = keep + partner(send, 1)
    total, inner, outer = lax.optimization_barrier((total, inner, outer))
    inner = partner(inner, 1)
    across = [(i, i + 1) for i in range(1, devices - 1, 2)]
    outer = lax.ppermute(outer, AXES, across + [(j, i) for i, j in across])
    length = samples + LANES
    shifted, both, low = pl.pallas_call(
        channels_kernel,
        out_shape=[
            jax.ShapeDtypeStruct((LAGS // STEP * channels, length), BF16),
            jax.ShapeDtypeStruct((2 * LANES, 2 * LANES), BF16),
            jax.ShapeDtypeStruct((LANES, 2 * LANES), BF16),
        ],
        in_specs=[VMEM] * 3 + [HBM] * 2,
        out_specs=[VMEM] * 3,
        scratch_shapes=[
            pltpu.SMEM(fir_taps.shape, F32),
            pltpu.SMEM(space_taps.shape, F32),
            pltpu.SemaphoreType.DMA((2,)),
        ],
        compiler_params=SMALL,
        name="channels",
    )(near, inner, outer, in_hbm(fir_taps), in_hbm(space_taps))
    distance = 2
    while distance < devices:
        if distance == 16:
            total, shifted, both, low = lax.optimization_barrier((total, shifted, both, low))
        total = total + partner(total, distance)
        distance *= 2
    other = partner(total, 1)
    return pl.pallas_call(
        correlate_kernel,
        out_shape=jax.ShapeDtypeStruct((PANELS, SRC, channels, LAGS), F32),
        in_specs=[VMEM] * 5,
        out_specs=VMEM,
        compiler_params=SMALL,
        name="correlate",
    )(total, other, shifted, both, low)


def solution(mesh):
    return jax.shard_map(
        local,
        mesh=mesh,
        in_specs=(P(AXES, None), P(), P(), P()),
        out_specs=P(None, None, AXES, None),
        check_vma=False,
    )
```

```python
import functools

import jax
import jax.numpy as jnp
from jax import lax
from jax.experimental import pallas as pl
from jax.experimental.pallas import tpu as pltpu
from jax.sharding import PartitionSpec as P

RUN = 64
LAGS = 256
PANELS = 3
SRC = 4
AXES = ("fibre", "seg")
LANES = 128
STEP = 16
HALO = 16
ROWS = PANELS * SRC
HALF_ROWS = ROWS // 2
VMEM = pl.BlockSpec(memory_space=pltpu.VMEM)
HBM = pl.BlockSpec(memory_space=pltpu.HBM)
SMALL = pltpu.CompilerParams(vmem_limit_bytes=16 * 2**20)
BF16 = jnp.bfloat16
F32 = jnp.float32


def split(x):
    high = x.astype(BF16)
    return high, (x - high.astype(F32)).astype(BF16)


def split_rows(x):
    high = x.astype(BF16).astype(F32)
    return jnp.concatenate([high, x - high, high], axis=0).astype(BF16)


def split_columns(x):
    high = x.astype(BF16).astype(F32)
    return jnp.concatenate([high, high, x - high], axis=1).astype(BF16)


def taps_at(taps_ref, index):
    total = jnp.zeros(index.shape, F32)
    for j in range(taps_ref.shape[0]):
        total = jnp.where(index == j, taps_ref[j], total)
    return total


def fir_matrix(fir_ref):
    lane = lax.broadcasted_iota(jnp.int32, (8, LANES), 1)
    row = lax.broadcasted_iota(jnp.int32, (8, LANES), 0)
    first = taps_at(fir_ref, lane - row)
    first = jnp.concatenate([first, jnp.zeros_like(first)], axis=1)
    return jnp.concatenate(
        [first if g == 0 else pltpu.roll(first, 8 * g, 1) for g in range(LANES // 8)], axis=0
    )


def to_blocks(x):
    return jnp.concatenate(
        [x[:, k : k + LANES] for k in range(0, x.shape[1], LANES)], axis=0
    )


def from_blocks(x, rows):
    return jnp.concatenate([x[k : k + rows] for k in range(0, x.shape[0], rows)], axis=1)


def earlier(x, rows):
    return jnp.concatenate([jnp.zeros((rows, x.shape[1]), x.dtype), x[:-rows]], axis=0)


def later(x, rows):
    return jnp.concatenate([x[rows:], jnp.zeros((rows, x.shape[1]), x.dtype)], axis=0)


def filter_and_norm(x, fir_both, fir_low):
    rows, samples = x.shape
    high, low = split(to_blocks(x))
    dot = functools.partial(jnp.dot, preferred_element_type=F32)
    full = dot(jnp.concatenate([high, low], axis=1), fir_both) + dot(high, fir_low)
    smooth = full[:, :LANES] + earlier(full[:, LANES:], rows)
    high, low = split(jnp.abs(smooth))
    u = lax.broadcasted_iota(jnp.int32, (2 * LANES, LANES), 0) % LANES
    t = lax.broadcasted_iota(jnp.int32, (2 * LANES, LANES), 1)
    bands = [jnp.abs(u - t) <= RUN, u - t >= LANES - RUN, t - u >= LANES - RUN]
    window = jnp.concatenate([jnp.where(b, 1.0, 0.0).astype(BF16) for b in bands], axis=1)
    sums = dot(jnp.concatenate([high, low], axis=1), window)
    total = (
        sums[:, :LANES]
        + earlier(sums[:, LANES : 2 * LANES], rows)
        + later(sums[:, 2 * LANES :], rows)
    )
    shape = total.shape
    where = lax.broadcasted_iota(jnp.int32, shape, 0) // rows * LANES
    where = where + lax.broadcasted_iota(jnp.int32, shape, 1)
    count = jnp.minimum(where, RUN) + jnp.minimum(samples - 1 - where, RUN) + 1
    level = total / count.astype(F32)
    return from_blocks(smooth / (level + 1e-5), rows)


def pack(x):
    width = x.shape[1] // 4
    tail = x[:, 3 * width :]
    more = [
        jnp.concatenate([tail[k : k + 1] for k in range(3 * g, 3 * g + 3)], axis=1)
        for g in range(2)
    ]
    return jnp.concatenate([x[:, : 3 * width]] + more, axis=0)


def unpack(x):
    width = x.shape[1] // 3
    tail = [x[6 + k // 3 : 7 + k // 3, k % 3 * width : (k % 3 + 1) * width] for k in range(6)]
    return jnp.concatenate([x[:6], jnp.concatenate(tail, axis=0)], axis=1)


def parity(number):
    total = 0
    for k in range(16):
        total = total ^ (number >> k)
    return total & 1


def fetch(pairs, sems):
    copies = [pltpu.make_async_copy(a, b, sems.at[i]) for i, (a, b) in enumerate(pairs)]
    for copy in copies:
        copy.start()
    return copies


def share_kernel(
    strain_hbm,
    space_hbm,
    sources_hbm,
    keep_ref,
    send_ref,
    inner_ref,
    outer_ref,
    strain_ref,
    space_ref,
    sources_ref,
    sems,
):
    copies = fetch(
        [(sources_hbm, sources_ref), (space_hbm, space_ref), (strain_hbm, strain_ref)], sems
    )
    channels = strain_ref.shape[0]
    me = lax.axis_index(AXES)
    mine = parity(me)
    half_span = (space_ref.shape[0] - 1) // 2
    even = me % 2 == 0
    copies[0].wait()
    row = lax.broadcasted_iota(jnp.int32, (16, channels), 0)
    lane = lax.broadcasted_iota(jnp.int32, (16, channels), 1)
    source = jnp.full((16, channels), -(1 << 20), jnp.int32)
    for k in range(ROWS):
        half = mine if k < HALF_ROWS else 1 - mine
        number = half * HALF_ROWS + k % HALF_ROWS
        place = k if k < HALF_ROWS else k - HALF_ROWS + 8
        source = jnp.where(row == place, sources_ref[number // SRC, number % SRC], source)
    copies[1].wait()
    matrix = taps_at(space_ref, lane + me * channels - source + half_span)
    copies[2].wait()
    x = strain_ref[...]
    inner_ref[...] = jnp.where(even, x[channels - HALO :], x[:HALO])
    outer_ref[...] = jnp.where(even, x[:HALO], x[channels - HALO :])
    share = jnp.dot(split_columns(matrix), split_rows(x), preferred_element_type=F32)
    keep_ref[...] = pack(share[:HALF_ROWS])
    send_ref[...] = pack(share[8 : 8 + HALF_ROWS])


def channels_kernel(
    strain_ref,
    inner_ref,
    outer_ref,
    fir_hbm,
    space_hbm,
    shifted_ref,
    both_ref,
    low_ref,
    fir_ref,
    space_ref,
    sems,
):
    copies = fetch([(space_hbm, space_ref), (fir_hbm, fir_ref)], sems)
    channels, samples = strain_ref.shape
    half_span = (space_ref.shape[0] - 1) // 2
    me = lax.axis_index(AXES)
    even = me % 2 == 0
    inner, outer = inner_ref[...], outer_ref[...]
    outer = jnp.where((me == 0) | (me == lax.axis_size(AXES) - 1), 0.0, outer)
    before, after = jnp.where(even, outer, inner), jnp.where(even, inner, outer)
    x = jnp.concatenate([before, strain_ref[...], after], axis=0)
    wide = x.shape[0]
    row = lax.broadcasted_iota(jnp.int32, (channels, wide), 0)
    column = lax.broadcasted_iota(jnp.int32, (channels, wide), 1)
    copies[0].wait()
    matrix = taps_at(space_ref, column - HALO - row + half_span)
    spaced = jnp.dot(split_columns(matrix), split_rows(x), preferred_element_type=F32)
    copies[1].wait()
    high, low = split(fir_matrix(fir_ref))
    both = jnp.concatenate([high, high], axis=0)
    both_ref[...] = both
    low_ref[...] = low
    normed = filter_and_norm(spaced, both, low)
    length = shifted_ref.shape[1]
    padded = jnp.concatenate(
        [
            jnp.zeros((channels, LANES), F32),
            normed,
            jnp.zeros((channels, 2 * LANES), F32),
        ],
        axis=1,
    )
    per_tile = LANES // STEP
    for q in range(0, per_tile, 2):
        turned = [
            padded if k == 0 else pltpu.roll(padded, padded.shape[1] - STEP * k, 1)
            for k in (q, q + 1)
        ]
        pair = jnp.concatenate(turned, axis=0).astype(BF16)
        for h in range(LAGS // LANES):
            at = (h * per_tile + q) * channels
            shifted_ref[at : at + 2 * channels, :] = pair[:, h * LANES : h * LANES + length]


def swap(upper, lower, distance, lane):
    near = (lane // distance) % 2 == 0
    return (
        jnp.where(near, upper, pltpu.roll(lower, distance, 1)),
        jnp.where(near, pltpu.roll(upper, LANES - distance, 1), lower),
    )


def correlate_kernel(mine_ref, other_ref, shifted_ref, both_ref, low_ref, out_ref):
    channels = out_ref.shape[2]
    mine = unpack(mine_ref[...])
    other = unpack(other_ref[...])
    samples = mine.shape[1]
    even = parity(lax.axis_index(AXES)) == 0
    spaced = jnp.concatenate(
        [
            jnp.where(even, mine, other),
            jnp.where(even, other, mine),
            jnp.zeros((16 - ROWS, samples), F32),
        ],
        axis=0,
    )
    normed = filter_and_norm(spaced, both_ref[...], low_ref[...])
    normed = normed.astype(BF16).astype(F32)
    padded = jnp.concatenate([normed, jnp.zeros((16, LANES), F32)], axis=1)
    lane = lax.broadcasted_iota(jnp.int32, (STEP, LANES), 1)
    row = lax.broadcasted_iota(jnp.int32, (STEP, LANES), 0)
    straight = lane >= row
    records = []
    for k in range(ROWS):
        one = jnp.broadcast_to(padded[k : k + 1], (STEP, padded.shape[1]))
        tiles = [
            pltpu.roll(one[:, j : j + LANES], 0, 1, stride=1, stride_axis=0)
            for j in range(0, padded.shape[1], LANES)
        ]
        previous = [tiles[-1]] + tiles[:-1]
        records.append(
            jnp.concatenate(
                [jnp.where(straight, b, a) for a, b in zip(previous, tiles)], axis=1
            ).astype(BF16)
        )
    records = jnp.concatenate(records, axis=0)
    result = lax.dot_general(
        shifted_ref[...], records, (((1,), (1,)), ((), ())), preferred_element_type=F32
    )
    result = result * float(samples) ** -0.5
    result = jnp.concatenate(
        [result, jnp.zeros((result.shape[0], 2 * LANES - result.shape[1]), F32)], axis=1
    )
    per_tile = LANES // STEP
    lane = lax.broadcasted_iota(jnp.int32, (channels, LANES), 1)
    for h in range(LAGS // LANES):
        for tile in range(2):
            parts = [
                result[
                    (h * per_tile + q) * channels : (h * per_tile + q + 1) * channels,
                    tile * LANES : (tile + 1) * LANES,
                ]
                for q in range(per_tile)
            ]
            for distance in (4, 2, 1):
                for q in range(per_tile):
                    if q & distance == 0:
                        parts[q], parts[q + distance] = swap(
                            parts[q], parts[q + distance], distance * STEP, lane
                        )
            for q in range(per_tile):
                number = tile * per_tile + q
                if number < ROWS:
                    out_ref[number // SRC, number % SRC, :, h * LANES : (h + 1) * LANES] = parts[q]


def in_hbm(x):
    return pltpu.with_memory_space_constraint(x, pltpu.HBM)


def channels_call(near, inner, outer, fir_taps, space_taps):
    channels, samples = near.shape
    length = samples + LANES
    return pl.pallas_call(
        channels_kernel,
        out_shape=[
            jax.ShapeDtypeStruct((LAGS // STEP * channels, length), BF16),
            jax.ShapeDtypeStruct((2 * LANES, 2 * LANES), BF16),
            jax.ShapeDtypeStruct((LANES, 2 * LANES), BF16),
        ],
        in_specs=[VMEM] * 3 + [HBM] * 2,
        out_specs=[VMEM] * 3,
        scratch_shapes=[
            pltpu.SMEM(fir_taps.shape, F32),
            pltpu.SMEM(space_taps.shape, F32),
            pltpu.SemaphoreType.DMA((2,)),
        ],
        compiler_params=SMALL,
        name="channels",
    )(near, inner, outer, in_hbm(fir_taps), in_hbm(space_taps))


def local(strain, fir_taps, space_taps, sources):
    channels, samples = strain.shape
    devices = lax.axis_size(AXES)
    packed = jax.ShapeDtypeStruct((8, samples * 3 // 4), F32)
    edge = jax.ShapeDtypeStruct((HALO, samples), F32)
    near = jax.ShapeDtypeStruct(strain.shape, F32)
    keep, send, inner, outer, near = pl.pallas_call(
        share_kernel,
        out_shape=[packed, packed, edge, edge, near],
        in_specs=[HBM] * 3,
        out_specs=[VMEM] * 5,
        scratch_shapes=[
            pltpu.SMEM(space_taps.shape, F32),
            pltpu.SMEM(sources.shape, jnp.int32),
            pltpu.SemaphoreType.DMA((3,)),
        ],
        compiler_params=SMALL,
        name="share",
    )(*[in_hbm(x) for x in (strain, space_taps, sources)])

    def partner(x, distance):
        return lax.ppermute(x, AXES, [(i, i ^ distance) for i in range(devices)])

    total = keep + partner(send, 1)
    across = [(i, i + 1) for i in range(1, devices - 1, 2)] + [(0, devices - 1)]
    across = across + [(j, i) for i, j in across]
    steps = [1 << k for k in range(1, devices.bit_length() - 1)]
    order = steps[-1:] + steps[1:-1][:1] + steps[:1] + steps[2:-1]
    for place, distance in enumerate(order):
        if place == 0:
            total, inner, outer = lax.optimization_barrier((total, inner, outer))
            inner = partner(inner, 1)
            outer = lax.ppermute(outer, AXES, across)
        if place == 2:
            shifted, both, low = channels_call(near, inner, outer, fir_taps, space_taps)
        if place == 3:
            total, shifted, both, low = lax.optimization_barrier((total, shifted, both, low))
        total = total + partner(total, distance + 1)
    other = partner(total, 1)
    return pl.pallas_call(
        correlate_kernel,
        out_shape=jax.ShapeDtypeStruct((PANELS, SRC, channels, LAGS), F32),
        in_specs=[VMEM] * 5,
        out_specs=VMEM,
        compiler_params=SMALL,
        name="correlate",
    )(total, other, shifted, both, low)


def solution(mesh):
    return jax.shard_map(
        local,
        mesh=mesh,
        in_specs=(P(AXES, None), P(), P(), P()),
        out_specs=P(None, None, AXES, None),
        check_vma=False,
    )
```

```python
import functools

import jax
import jax.numpy as jnp
from jax import lax
from jax.experimental import pallas as pl
from jax.experimental.pallas import tpu as pltpu
from jax.sharding import PartitionSpec as P

RUN = 64
LAGS = 256
PANELS = 3
SRC = 4
AXES = ("fibre", "seg")
LANES = 128
STEP = 32
HALO = 16
ROWS = PANELS * SRC
HALF_ROWS = ROWS // 2
VMEM = pl.BlockSpec(memory_space=pltpu.VMEM)
HBM = pl.BlockSpec(memory_space=pltpu.HBM)
SMALL = pltpu.CompilerParams(vmem_limit_bytes=16 * 2**20)
BF16 = jnp.bfloat16
F32 = jnp.float32


def split(x):
    high = x.astype(BF16)
    return high, (x - high.astype(F32)).astype(BF16)


def split_rows(x):
    high = x.astype(BF16).astype(F32)
    return jnp.concatenate([high, x - high, high], axis=0).astype(BF16)


def split_columns(x):
    high = x.astype(BF16).astype(F32)
    return jnp.concatenate([high, high, x - high], axis=1).astype(BF16)


def taps_at(taps_ref, index):
    total = jnp.zeros(index.shape, F32)
    for j in range(taps_ref.shape[0]):
        total = jnp.where(index == j, taps_ref[j], total)
    return total


def fir_matrix(fir_ref):
    lane = lax.broadcasted_iota(jnp.int32, (8, LANES), 1)
    row = lax.broadcasted_iota(jnp.int32, (8, LANES), 0)
    first = taps_at(fir_ref, lane - row)
    first = jnp.concatenate([first, jnp.zeros_like(first)], axis=1)
    return jnp.concatenate(
        [first if g == 0 else pltpu.roll(first, 8 * g, 1) for g in range(LANES // 8)], axis=0
    )


def to_blocks(x):
    return jnp.concatenate(
        [x[:, k : k + LANES] for k in range(0, x.shape[1], LANES)], axis=0
    )


def from_blocks(x, rows):
    return jnp.concatenate([x[k : k + rows] for k in range(0, x.shape[0], rows)], axis=1)


def earlier(x, rows):
    return jnp.concatenate([jnp.zeros((rows, x.shape[1]), x.dtype), x[:-rows]], axis=0)


def later(x, rows):
    return jnp.concatenate([x[rows:], jnp.zeros((rows, x.shape[1]), x.dtype)], axis=0)


def window_bands():
    u = lax.broadcasted_iota(jnp.int32, (2 * LANES, LANES), 0) % LANES
    t = lax.broadcasted_iota(jnp.int32, (2 * LANES, LANES), 1)
    bands = [jnp.abs(u - t) <= RUN, u - t >= LANES - RUN, t - u >= LANES - RUN]
    return jnp.concatenate([jnp.where(b, 1.0, 0.0).astype(BF16) for b in bands], axis=1)


def filter_and_norm(x, fir_both, fir_low, window):
    rows, samples = x.shape
    high, low = split(to_blocks(x))
    dot = functools.partial(jnp.dot, preferred_element_type=F32)
    full = dot(jnp.concatenate([high, low], axis=1), fir_both) + dot(high, fir_low)
    smooth = full[:, :LANES] + earlier(full[:, LANES:], rows)
    high, low = split(jnp.abs(smooth))
    sums = dot(jnp.concatenate([high, low], axis=1), window)
    total = (
        sums[:, :LANES]
        + earlier(sums[:, LANES : 2 * LANES], rows)
        + later(sums[:, 2 * LANES :], rows)
    )
    shape = total.shape
    where = lax.broadcasted_iota(jnp.int32, shape, 0) // rows * LANES
    where = where + lax.broadcasted_iota(jnp.int32, shape, 1)
    count = jnp.minimum(where, RUN) + jnp.minimum(samples - 1 - where, RUN) + 1
    level = total / count.astype(F32)
    return from_blocks(smooth / (level + 1e-5), rows)


def pack(x):
    width = x.shape[1] // 4
    tail = x[:, 3 * width :]
    more = [
        jnp.concatenate([tail[k : k + 1] for k in range(3 * g, 3 * g + 3)], axis=1)
        for g in range(2)
    ]
    return jnp.concatenate([x[:, : 3 * width]] + more, axis=0)


def unpack(x):
    width = x.shape[1] // 3
    tail = [x[6 + k // 3 : 7 + k // 3, k % 3 * width : (k % 3 + 1) * width] for k in range(6)]
    return jnp.concatenate([x[:6], jnp.concatenate(tail, axis=0)], axis=1)


def parity(number):
    total = 0
    for k in range(16):
        total = total ^ (number >> k)
    return total & 1


def fetch(pairs, sems):
    copies = [pltpu.make_async_copy(a, b, sems.at[i]) for i, (a, b) in enumerate(pairs)]
    for copy in copies:
        copy.start()
    return copies


def share_kernel(
    strain_hbm,
    space_hbm,
    sources_hbm,
    keep_ref,
    send_ref,
    inner_ref,
    outer_ref,
    strain_ref,
    space_ref,
    sources_ref,
    sems,
):
    copies = fetch(
        [(sources_hbm, sources_ref), (space_hbm, space_ref), (strain_hbm, strain_ref)], sems
    )
    channels = strain_ref.shape[0]
    me = lax.axis_index(AXES)
    mine = parity(me)
    half_span = (space_ref.shape[0] - 1) // 2
    even = me % 2 == 0
    copies[0].wait()
    row = lax.broadcasted_iota(jnp.int32, (16, channels), 0)
    lane = lax.broadcasted_iota(jnp.int32, (16, channels), 1)
    source = jnp.full((16, channels), -(1 << 20), jnp.int32)
    for k in range(ROWS):
        half = mine if k < HALF_ROWS else 1 - mine
        number = half * HALF_ROWS + k % HALF_ROWS
        place = k if k < HALF_ROWS else k - HALF_ROWS + 8
        source = jnp.where(row == place, sources_ref[number // SRC, number % SRC], source)
    copies[1].wait()
    matrix = taps_at(space_ref, lane + me * channels - source + half_span)
    copies[2].wait()
    x = strain_ref[...]
    inner_ref[...] = jnp.where(even, x[channels - HALO :], x[:HALO])
    outer_ref[...] = jnp.where(even, x[:HALO], x[channels - HALO :])
    share = jnp.dot(split_columns(matrix), split_rows(x), preferred_element_type=F32)
    keep_ref[...] = pack(share[:HALF_ROWS])
    send_ref[...] = pack(share[8 : 8 + HALF_ROWS])


def tables_kernel(
    fir_hbm, space_hbm, space_matrix_ref, both_ref, low_ref, window_ref, fir_ref, space_ref, sems
):
    copies = fetch([(space_hbm, space_ref), (fir_hbm, fir_ref)], sems)
    window_ref[...] = window_bands()
    channels = space_matrix_ref.shape[0]
    half_span = (space_ref.shape[0] - 1) // 2
    row = lax.broadcasted_iota(jnp.int32, (channels, channels + 2 * HALO), 0)
    column = lax.broadcasted_iota(jnp.int32, (channels, channels + 2 * HALO), 1)
    copies[0].wait()
    space_matrix_ref[...] = split_columns(taps_at(space_ref, column - HALO - row + half_span))
    copies[1].wait()
    high, low = split(fir_matrix(fir_ref))
    both_ref[...] = jnp.concatenate([high, high], axis=0)
    low_ref[...] = low


def channels_kernel(
    strain_ref,
    inner_ref,
    outer_ref,
    space_matrix_ref,
    both_ref,
    low_ref,
    window_ref,
    shifted_ref,
):
    channels, samples = strain_ref.shape
    me = lax.axis_index(AXES)
    even = me % 2 == 0
    inner, outer = inner_ref[...], outer_ref[...]
    outer = jnp.where((me == 0) | (me == lax.axis_size(AXES) - 1), 0.0, outer)
    before, after = jnp.where(even, outer, inner), jnp.where(even, inner, outer)
    x = jnp.concatenate([before, strain_ref[...], after], axis=0)
    spaced = jnp.dot(space_matrix_ref[...], split_rows(x), preferred_element_type=F32)
    normed = filter_and_norm(spaced, both_ref[...], low_ref[...], window_ref[...])
    length = shifted_ref.shape[1]
    padded = jnp.concatenate(
        [
            jnp.zeros((channels, LANES), F32),
            normed,
            jnp.zeros((channels, 2 * LANES), F32),
        ],
        axis=1,
    )
    per_tile = LANES // STEP
    for q in range(0, per_tile, 2):
        turned = [
            padded if k == 0 else pltpu.roll(padded, padded.shape[1] - STEP * k, 1)
            for k in (q, q + 1)
        ]
        pair = jnp.concatenate(turned, axis=0).astype(BF16)
        for h in range(LAGS // LANES):
            at = (h * per_tile + q) * channels
            shifted_ref[at : at + 2 * channels, :] = pair[:, h * LANES : h * LANES + length]


def swap(upper, lower, distance, lane):
    near = (lane // distance) % 2 == 0
    return (
        jnp.where(near, upper, pltpu.roll(lower, distance, 1)),
        jnp.where(near, pltpu.roll(upper, LANES - distance, 1), lower),
    )


def lag_sums(shifted_ref, normed):
    rows = HALF_ROWS
    samples = normed.shape[1]
    coarse = LAGS // STEP
    channels = shifted_ref.shape[0] // coarse
    padded = jnp.concatenate([normed, jnp.zeros((normed.shape[0], LANES), F32)], axis=1)
    lane = lax.broadcasted_iota(jnp.int32, (STEP, LANES), 1)
    row = lax.broadcasted_iota(jnp.int32, (STEP, LANES), 0)
    straight = lane >= row
    records = []
    for k in range(rows):
        one = jnp.broadcast_to(padded[k : k + 1], (STEP, padded.shape[1]))
        tiles = [
            pltpu.roll(one[:, j : j + LANES], 0, 1, stride=1, stride_axis=0)
            for j in range(0, padded.shape[1], LANES)
        ]
        previous = [tiles[-1]] + tiles[:-1]
        records.append(
            jnp.concatenate(
                [jnp.where(straight, b, a) for a, b in zip(previous, tiles)], axis=1
            ).astype(BF16)
        )
    records = jnp.concatenate(records, axis=0)
    result = lax.dot_general(
        shifted_ref[...], records, (((1,), (1,)), ((), ())), preferred_element_type=F32
    )
    result = result * float(samples) ** -0.5
    per_tile = LANES // STEP
    tiles = -(-rows // per_tile)
    short = tiles * LANES - result.shape[1]
    if short:
        result = jnp.concatenate([result, jnp.zeros((result.shape[0], short), F32)], axis=1)
    lane = lax.broadcasted_iota(jnp.int32, (channels, LANES), 1)
    sums = [[None] * (LAGS // LANES) for _ in range(rows)]
    for h in range(LAGS // LANES):
        for tile in range(tiles):
            parts = [
                result[
                    (h * per_tile + q) * channels : (h * per_tile + q + 1) * channels,
                    tile * LANES : (tile + 1) * LANES,
                ]
                for q in range(per_tile)
            ]
            for distance in [d for d in (8, 4, 2, 1) if d < per_tile]:
                for q in range(per_tile):
                    if q & distance == 0:
                        parts[q], parts[q + distance] = swap(
                            parts[q], parts[q + distance], distance * STEP, lane
                        )
            for q in range(per_tile):
                if tile * per_tile + q < rows:
                    sums[tile * per_tile + q][h] = parts[q]
    return sums


def norm_kernel(total_ref, both_ref, low_ref, window_ref, normed_ref):
    spaced = unpack(total_ref[...])
    samples = spaced.shape[1]
    spaced = jnp.concatenate([spaced, jnp.zeros((8 - HALF_ROWS, samples), F32)], axis=0)
    normed = filter_and_norm(spaced, both_ref[...], low_ref[...], window_ref[...])
    normed = jnp.concatenate([normed[:, : samples // 2], normed[:, samples // 2 :]], axis=0)
    normed_ref[...] = normed.astype(BF16)


def rows_of(normed_ref):
    x = normed_ref[...].astype(F32)
    return jnp.concatenate([x[:8], x[8:]], axis=1)


def first_kernel(normed_ref, shifted_ref, sums_ref):
    for k, halves in enumerate(lag_sums(shifted_ref, rows_of(normed_ref))):
        for h, part in enumerate(halves):
            sums_ref[k, :, h * LANES : (h + 1) * LANES] = part


def second_kernel(normed_ref, shifted_ref, sums_ref, out_hbm, more_ref, sems):
    mine = parity(lax.axis_index(AXES))
    early = pltpu.make_async_copy(
        sums_ref, out_hbm.at[pl.ds(mine * HALF_ROWS, HALF_ROWS)], sems.at[0]
    )
    early.start()
    for k, halves in enumerate(lag_sums(shifted_ref, rows_of(normed_ref))):
        for h, part in enumerate(halves):
            more_ref[k, :, h * LANES : (h + 1) * LANES] = part
    late = pltpu.make_async_copy(
        more_ref, out_hbm.at[pl.ds((1 - mine) * HALF_ROWS, HALF_ROWS)], sems.at[1]
    )
    late.start()
    early.wait()
    late.wait()


def in_hbm(x):
    return pltpu.with_memory_space_constraint(x, pltpu.HBM)


def local(strain, fir_taps, space_taps, sources):
    channels, samples = strain.shape
    devices = lax.axis_size(AXES)
    packed = jax.ShapeDtypeStruct((8, samples * 3 // 4), F32)
    edge = jax.ShapeDtypeStruct((HALO, samples), F32)
    near = jax.ShapeDtypeStruct(strain.shape, F32)
    keep, send, inner, outer, near = pl.pallas_call(
        share_kernel,
        out_shape=[packed, packed, edge, edge, near],
        in_specs=[HBM] * 3,
        out_specs=[VMEM] * 5,
        scratch_shapes=[
            pltpu.SMEM(space_taps.shape, F32),
            pltpu.SMEM(sources.shape, jnp.int32),
            pltpu.SemaphoreType.DMA((3,)),
        ],
        compiler_params=SMALL,
        name="share",
    )(*[in_hbm(x) for x in (strain, space_taps, sources)])

    def partner(x, distance):
        return lax.ppermute(x, AXES, [(i, i ^ distance) for i in range(devices)])

    total = keep + partner(send, 1)
    across = [(i, i + 1) for i in range(1, devices - 1, 2)] + [(0, devices - 1)]
    across = across + [(j, i) for i, j in across]
    steps = [1 << k for k in range(1, devices.bit_length() - 1)]
    order = steps[-1:] + steps[1:-1][:1] + steps[:1] + steps[2:-1]
    for place, distance in enumerate(order):
        if place == 0:
            total, inner, outer = lax.optimization_barrier((total, inner, outer))
            inner = partner(inner, 1)
            outer = lax.ppermute(outer, AXES, across)
        if place == 1:
            total, fir_taps, space_taps = lax.optimization_barrier((total, fir_taps, space_taps))
            tables = pl.pallas_call(
                tables_kernel,
                out_shape=[
                    jax.ShapeDtypeStruct((channels, 3 * (channels + 2 * HALO)), BF16),
                    jax.ShapeDtypeStruct((2 * LANES, 2 * LANES), BF16),
                    jax.ShapeDtypeStruct((LANES, 2 * LANES), BF16),
                    jax.ShapeDtypeStruct((2 * LANES, 3 * LANES), BF16),
                ],
                in_specs=[HBM] * 2,
                out_specs=[VMEM] * 4,
                scratch_shapes=[
                    pltpu.SMEM(fir_taps.shape, F32),
                    pltpu.SMEM(space_taps.shape, F32),
                    pltpu.SemaphoreType.DMA((2,)),
                ],
                compiler_params=SMALL,
                name="tables",
            )(in_hbm(fir_taps), in_hbm(space_taps))
        if place == 2:
            total, *tables = lax.optimization_barrier((total, *tables))
            shifted = pl.pallas_call(
                channels_kernel,
                out_shape=jax.ShapeDtypeStruct(
                    (LAGS // STEP * channels, samples + LANES), BF16
                ),
                in_specs=[VMEM] * 7,
                out_specs=VMEM,
                compiler_params=SMALL,
                name="channels",
            )(near, inner, outer, *tables)
        if place == 3:
            total, shifted = lax.optimization_barrier((total, shifted))
        total = total + partner(total, distance + 1)
    mine = pl.pallas_call(
        norm_kernel,
        out_shape=jax.ShapeDtypeStruct((16, samples // 2), BF16),
        in_specs=[VMEM] * 4,
        out_specs=VMEM,
        compiler_params=SMALL,
        name="norm",
    )(total, *tables[1:])
    other = partner(mine, 1)
    sums = jax.ShapeDtypeStruct((HALF_ROWS, channels, LAGS), F32)
    first = pl.pallas_call(
        first_kernel,
        out_shape=sums,
        in_specs=[VMEM] * 2,
        out_specs=VMEM,
        compiler_params=SMALL,
        name="first",
    )(mine, shifted)
    out = pl.pallas_call(
        second_kernel,
        out_shape=jax.ShapeDtypeStruct((ROWS, channels, LAGS), F32),
        in_specs=[VMEM] * 3,
        out_specs=HBM,
        scratch_shapes=[pltpu.VMEM(sums.shape, F32), pltpu.SemaphoreType.DMA((2,))],
        compiler_params=SMALL,
        name="second",
    )(other, shifted, first)
    return out.reshape(PANELS, SRC, channels, LAGS)


def solution(mesh):
    return jax.shard_map(
        local,
        mesh=mesh,
        in_specs=(P(AXES, None), P(), P(), P()),
        out_specs=P(None, None, AXES, None),
        check_vma=False,
    )
```

```python
import functools

import jax
import jax.numpy as jnp
from jax import lax
from jax.experimental import pallas as pl
from jax.experimental.pallas import tpu as pltpu
from jax.sharding import PartitionSpec as P

RUN = 64
LAGS = 256
PANELS = 3
SRC = 4
AXES = ("fibre", "seg")
LANES = 128
STEP = 32
HALO = 16
ROWS = PANELS * SRC
HALF_ROWS = ROWS // 2
VMEM = pl.BlockSpec(memory_space=pltpu.VMEM)
HBM = pl.BlockSpec(memory_space=pltpu.HBM)
SMALL = pltpu.CompilerParams(vmem_limit_bytes=16 * 2**20)
BF16 = jnp.bfloat16
F32 = jnp.float32


def split(x):
    high = x.astype(BF16)
    return high, (x - high.astype(F32)).astype(BF16)


def split_rows(x):
    high = x.astype(BF16).astype(F32)
    return jnp.concatenate([high, x - high, high], axis=0).astype(BF16)


def split_columns(x):
    high = x.astype(BF16).astype(F32)
    return jnp.concatenate([high, high, x - high], axis=1).astype(BF16)


def taps_at(taps_ref, index):
    total = jnp.zeros(index.shape, F32)
    for j in range(taps_ref.shape[0]):
        total = jnp.where(index == j, taps_ref[j], total)
    return total


def fir_matrix(fir_ref):
    lane = lax.broadcasted_iota(jnp.int32, (8, LANES), 1)
    row = lax.broadcasted_iota(jnp.int32, (8, LANES), 0)
    first = taps_at(fir_ref, lane - row)
    first = jnp.concatenate([first, jnp.zeros_like(first)], axis=1)
    return jnp.concatenate(
        [first if g == 0 else pltpu.roll(first, 8 * g, 1) for g in range(LANES // 8)], axis=0
    )


def to_blocks(x):
    return jnp.concatenate(
        [x[:, k : k + LANES] for k in range(0, x.shape[1], LANES)], axis=0
    )


def from_blocks(x, rows):
    return jnp.concatenate([x[k : k + rows] for k in range(0, x.shape[0], rows)], axis=1)


def earlier(x, rows):
    return jnp.concatenate([jnp.zeros((rows, x.shape[1]), x.dtype), x[:-rows]], axis=0)


def later(x, rows):
    return jnp.concatenate([x[rows:], jnp.zeros((rows, x.shape[1]), x.dtype)], axis=0)


def window_bands():
    u = lax.broadcasted_iota(jnp.int32, (2 * LANES, LANES), 0) % LANES
    t = lax.broadcasted_iota(jnp.int32, (2 * LANES, LANES), 1)
    bands = [jnp.abs(u - t) <= RUN, u - t >= LANES - RUN, t - u >= LANES - RUN]
    return jnp.concatenate([jnp.where(b, 1.0, 0.0).astype(BF16) for b in bands], axis=1)


def filter_and_norm(x, fir_both, fir_low, window):
    rows, samples = x.shape
    high, low = split(to_blocks(x))
    dot = functools.partial(jnp.dot, preferred_element_type=F32)
    full = dot(jnp.concatenate([high, low], axis=1), fir_both) + dot(high, fir_low)
    smooth = full[:, :LANES] + earlier(full[:, LANES:], rows)
    high, low = split(jnp.abs(smooth))
    sums = dot(jnp.concatenate([high, low], axis=1), window)
    total = (
        sums[:, :LANES]
        + earlier(sums[:, LANES : 2 * LANES], rows)
        + later(sums[:, 2 * LANES :], rows)
    )
    shape = total.shape
    where = lax.broadcasted_iota(jnp.int32, shape, 0) // rows * LANES
    where = where + lax.broadcasted_iota(jnp.int32, shape, 1)
    count = jnp.minimum(where, RUN) + jnp.minimum(samples - 1 - where, RUN) + 1
    level = total / count.astype(F32)
    return from_blocks(smooth / (level + 1e-5), rows)


def pack(x):
    width = x.shape[1] // 4
    tail = x[:, 3 * width :]
    more = [
        jnp.concatenate([tail[k : k + 1] for k in range(3 * g, 3 * g + 3)], axis=1)
        for g in range(2)
    ]
    return jnp.concatenate([x[:, : 3 * width]] + more, axis=0)


def unpack(x):
    width = x.shape[1] // 3
    tail = [x[6 + k // 3 : 7 + k // 3, k % 3 * width : (k % 3 + 1) * width] for k in range(6)]
    return jnp.concatenate([x[:6], jnp.concatenate(tail, axis=0)], axis=1)


def parity(number):
    total = 0
    for k in range(16):
        total = total ^ (number >> k)
    return total & 1


def fetch(pairs, sems):
    copies = [pltpu.make_async_copy(a, b, sems.at[i]) for i, (a, b) in enumerate(pairs)]
    for copy in copies:
        copy.start()
    return copies


def share_kernel(
    strain_hbm,
    space_hbm,
    sources_hbm,
    keep_ref,
    send_ref,
    inner_ref,
    outer_ref,
    strain_ref,
    space_ref,
    sources_ref,
    sems,
):
    copies = fetch(
        [(sources_hbm, sources_ref), (space_hbm, space_ref), (strain_hbm, strain_ref)], sems
    )
    channels = strain_ref.shape[0]
    me = lax.axis_index(AXES)
    mine = parity(me)
    half_span = (space_ref.shape[0] - 1) // 2
    even = me % 2 == 0
    copies[0].wait()
    row = lax.broadcasted_iota(jnp.int32, (16, channels), 0)
    lane = lax.broadcasted_iota(jnp.int32, (16, channels), 1)
    source = jnp.full((16, channels), -(1 << 20), jnp.int32)
    for k in range(ROWS):
        half = mine if k < HALF_ROWS else 1 - mine
        number = half * HALF_ROWS + k % HALF_ROWS
        place = k if k < HALF_ROWS else k - HALF_ROWS + 8
        source = jnp.where(row == place, sources_ref[number // SRC, number % SRC], source)
    copies[1].wait()
    matrix = taps_at(space_ref, lane + me * channels - source + half_span)
    copies[2].wait()
    x = strain_ref[...]
    inner_ref[...] = jnp.where(even, x[channels - HALO :], x[:HALO])
    outer_ref[...] = jnp.where(even, x[:HALO], x[channels - HALO :])
    share = jnp.dot(split_columns(matrix), split_rows(x), preferred_element_type=F32)
    keep_ref[...] = pack(share[:HALF_ROWS])
    send_ref[...] = pack(share[8 : 8 + HALF_ROWS])


def tables_kernel(
    fir_hbm, space_hbm, space_matrix_ref, both_ref, low_ref, window_ref, fir_ref, space_ref, sems
):
    copies = fetch([(space_hbm, space_ref), (fir_hbm, fir_ref)], sems)
    window_ref[...] = window_bands()
    channels = space_matrix_ref.shape[0]
    half_span = (space_ref.shape[0] - 1) // 2
    row = lax.broadcasted_iota(jnp.int32, (channels, channels + 2 * HALO), 0)
    column = lax.broadcasted_iota(jnp.int32, (channels, channels + 2 * HALO), 1)
    copies[0].wait()
    space_matrix_ref[...] = split_columns(taps_at(space_ref, column - HALO - row + half_span))
    copies[1].wait()
    high, low = split(fir_matrix(fir_ref))
    both_ref[...] = jnp.concatenate([high, high], axis=0)
    low_ref[...] = low


def channels_kernel(
    strain_ref,
    inner_ref,
    outer_ref,
    space_matrix_ref,
    both_ref,
    low_ref,
    window_ref,
    shifted_ref,
):
    channels, samples = strain_ref.shape
    me = lax.axis_index(AXES)
    even = me % 2 == 0
    inner, outer = inner_ref[...], outer_ref[...]
    outer = jnp.where((me == 0) | (me == lax.axis_size(AXES) - 1), 0.0, outer)
    before, after = jnp.where(even, outer, inner), jnp.where(even, inner, outer)
    x = jnp.concatenate([before, strain_ref[...], after], axis=0)
    spaced = jnp.dot(space_matrix_ref[...], split_rows(x), preferred_element_type=F32)
    normed = filter_and_norm(spaced, both_ref[...], low_ref[...], window_ref[...])
    length = shifted_ref.shape[1]
    padded = jnp.concatenate(
        [
            jnp.zeros((channels, LANES), F32),
            normed,
            jnp.zeros((channels, 2 * LANES), F32),
        ],
        axis=1,
    )
    per_tile = LANES // STEP
    for q in range(0, per_tile, 2):
        turned = [
            padded if k == 0 else pltpu.roll(padded, padded.shape[1] - STEP * k, 1)
            for k in (q, q + 1)
        ]
        pair = jnp.concatenate(turned, axis=0).astype(BF16)
        for h in range(LAGS // LANES):
            at = (h * per_tile + q) * channels
            shifted_ref[at : at + 2 * channels, :] = pair[:, h * LANES : h * LANES + length]


def swap(upper, lower, distance, lane):
    near = (lane // distance) % 2 == 0
    return (
        jnp.where(near, upper, pltpu.roll(lower, distance, 1)),
        jnp.where(near, pltpu.roll(upper, LANES - distance, 1), lower),
    )


def lag_sums(shifted_ref, normed):
    rows = HALF_ROWS
    samples = normed.shape[1]
    coarse = LAGS // STEP
    channels = shifted_ref.shape[0] // coarse
    padded = jnp.concatenate([normed, jnp.zeros((normed.shape[0], LANES), F32)], axis=1)
    lane = lax.broadcasted_iota(jnp.int32, (STEP, LANES), 1)
    row = lax.broadcasted_iota(jnp.int32, (STEP, LANES), 0)
    straight = lane >= row
    records = []
    for k in range(rows):
        one = jnp.broadcast_to(padded[k : k + 1], (STEP, padded.shape[1]))
        tiles = [
            pltpu.roll(one[:, j : j + LANES], 0, 1, stride=1, stride_axis=0)
            for j in range(0, padded.shape[1], LANES)
        ]
        previous = [tiles[-1]] + tiles[:-1]
        records.append(
            jnp.concatenate(
                [jnp.where(straight, b, a) for a, b in zip(previous, tiles)], axis=1
            ).astype(BF16)
        )
    records = jnp.concatenate(records, axis=0)
    result = lax.dot_general(
        shifted_ref[...], records, (((1,), (1,)), ((), ())), preferred_element_type=F32
    )
    result = result * float(samples) ** -0.5
    per_tile = LANES // STEP
    tiles = -(-rows // per_tile)
    short = tiles * LANES - result.shape[1]
    if short:
        result = jnp.concatenate([result, jnp.zeros((result.shape[0], short), F32)], axis=1)
    lane = lax.broadcasted_iota(jnp.int32, (channels, LANES), 1)
    sums = [[None] * (LAGS // LANES) for _ in range(rows)]
    for h in range(LAGS // LANES):
        for tile in range(tiles):
            parts = [
                result[
                    (h * per_tile + q) * channels : (h * per_tile + q + 1) * channels,
                    tile * LANES : (tile + 1) * LANES,
                ]
                for q in range(per_tile)
            ]
            for distance in [d for d in (8, 4, 2, 1) if d < per_tile]:
                for q in range(per_tile):
                    if q & distance == 0:
                        parts[q], parts[q + distance] = swap(
                            parts[q], parts[q + distance], distance * STEP, lane
                        )
            for q in range(per_tile):
                if tile * per_tile + q < rows:
                    sums[tile * per_tile + q][h] = parts[q]
    return sums


def norm_kernel(total_ref, both_ref, low_ref, window_ref, normed_ref):
    spaced = unpack(total_ref[...])
    samples = spaced.shape[1]
    spaced = jnp.concatenate([spaced, jnp.zeros((8 - HALF_ROWS, samples), F32)], axis=0)
    normed = filter_and_norm(spaced, both_ref[...], low_ref[...], window_ref[...])
    normed = jnp.concatenate([normed[:, : samples // 2], normed[:, samples // 2 :]], axis=0)
    normed_ref[...] = normed.astype(BF16)


def rows_of(normed_ref):
    x = normed_ref[...].astype(F32)
    return jnp.concatenate([x[:8], x[8:]], axis=1)


def first_kernel(normed_ref, shifted_ref, sums_ref):
    for k, halves in enumerate(lag_sums(shifted_ref, rows_of(normed_ref))):
        for h, part in enumerate(halves):
            sums_ref[k, :, h * LANES : (h + 1) * LANES] = part


def second_kernel(normed_ref, shifted_ref, sums_ref, out_hbm, more_ref, sems):
    mine = parity(lax.axis_index(AXES))
    early = pltpu.make_async_copy(
        sums_ref, out_hbm.at[pl.ds(mine * HALF_ROWS, HALF_ROWS)], sems.at[0]
    )
    early.start()
    for k, halves in enumerate(lag_sums(shifted_ref, rows_of(normed_ref))):
        for h, part in enumerate(halves):
            more_ref[k, :, h * LANES : (h + 1) * LANES] = part
    late = pltpu.make_async_copy(
        more_ref, out_hbm.at[pl.ds((1 - mine) * HALF_ROWS, HALF_ROWS)], sems.at[1]
    )
    late.start()
    early.wait()
    late.wait()


def in_hbm(x):
    return pltpu.with_memory_space_constraint(x, pltpu.HBM)


def local(strain, fir_taps, space_taps, sources):
    channels, samples = strain.shape
    devices = lax.axis_size(AXES)
    packed = jax.ShapeDtypeStruct((8, samples * 3 // 4), F32)
    edge = jax.ShapeDtypeStruct((HALO, samples), F32)
    near = jax.ShapeDtypeStruct(strain.shape, F32)
    keep, send, inner, outer, near = pl.pallas_call(
        share_kernel,
        out_shape=[packed, packed, edge, edge, near],
        in_specs=[HBM] * 3,
        out_specs=[VMEM] * 5,
        scratch_shapes=[
            pltpu.SMEM(space_taps.shape, F32),
            pltpu.SMEM(sources.shape, jnp.int32),
            pltpu.SemaphoreType.DMA((3,)),
        ],
        compiler_params=SMALL,
        name="share",
    )(*[in_hbm(x) for x in (strain, space_taps, sources)])

    def partner(x, distance):
        return lax.ppermute(x, AXES, [(i, i ^ distance) for i in range(devices)])

    total = keep + partner(send, 1)
    across = [(i, i + 1) for i in range(1, devices - 1, 2)] + [(0, devices - 1)]
    across = across + [(j, i) for i, j in across]
    steps = [1 << k for k in range(1, devices.bit_length() - 1)]
    order = [(distance + 1,) for distance in steps[:1:-1]] + [(5, 3, 6)]
    for place, masks in enumerate(order):
        if place == 0:
            total, inner = lax.optimization_barrier((total, inner))
            inner = partner(inner, 1)
            total, outer = lax.optimization_barrier((total, outer))
            outer = lax.ppermute(outer, AXES, across)
        if place == 1:
            total, fir_taps, space_taps = lax.optimization_barrier((total, fir_taps, space_taps))
            tables = pl.pallas_call(
                tables_kernel,
                out_shape=[
                    jax.ShapeDtypeStruct((channels, 3 * (channels + 2 * HALO)), BF16),
                    jax.ShapeDtypeStruct((2 * LANES, 2 * LANES), BF16),
                    jax.ShapeDtypeStruct((LANES, 2 * LANES), BF16),
                    jax.ShapeDtypeStruct((2 * LANES, 3 * LANES), BF16),
                ],
                in_specs=[HBM] * 2,
                out_specs=[VMEM] * 4,
                scratch_shapes=[
                    pltpu.SMEM(fir_taps.shape, F32),
                    pltpu.SMEM(space_taps.shape, F32),
                    pltpu.SemaphoreType.DMA((2,)),
                ],
                compiler_params=SMALL,
                name="tables",
            )(in_hbm(fir_taps), in_hbm(space_taps))
        if place == len(order) - 1:
            total, *tables = lax.optimization_barrier((total, *tables))
            shifted = pl.pallas_call(
                channels_kernel,
                out_shape=jax.ShapeDtypeStruct(
                    (LAGS // STEP * channels, samples + LANES), BF16
                ),
                in_specs=[VMEM] * 7,
                out_specs=VMEM,
                compiler_params=SMALL,
                name="channels",
            )(near, inner, outer, *tables)
        total = sum([partner(total, mask) for mask in masks], total)
    total, shifted = lax.optimization_barrier((total, shifted))
    mine = pl.pallas_call(
        norm_kernel,
        out_shape=jax.ShapeDtypeStruct((16, samples // 2), BF16),
        in_specs=[VMEM] * 4,
        out_specs=VMEM,
        compiler_params=SMALL,
        name="norm",
    )(total, *tables[1:])
    other = partner(mine, 1)
    sums = jax.ShapeDtypeStruct((HALF_ROWS, channels, LAGS), F32)
    first = pl.pallas_call(
        first_kernel,
        out_shape=sums,
        in_specs=[VMEM] * 2,
        out_specs=VMEM,
        compiler_params=SMALL,
        name="first",
    )(mine, shifted)
    out = pl.pallas_call(
        second_kernel,
        out_shape=jax.ShapeDtypeStruct((ROWS, channels, LAGS), F32),
        in_specs=[VMEM] * 3,
        out_specs=HBM,
        scratch_shapes=[pltpu.VMEM(sums.shape, F32), pltpu.SemaphoreType.DMA((2,))],
        compiler_params=SMALL,
        name="second",
    )(other, shifted, first)
    return out.reshape(PANELS, SRC, channels, LAGS)


def solution(mesh):
    return jax.shard_map(
        local,
        mesh=mesh,
        in_specs=(P(AXES, None), P(), P(), P()),
        out_specs=P(None, None, AXES, None),
        check_vma=False,
    )
```

```python
import functools

import jax
import jax.numpy as jnp
from jax import lax
from jax.experimental import pallas as pl
from jax.experimental.pallas import tpu as pltpu
from jax.sharding import PartitionSpec as P

RUN = 64
LAGS = 256
PANELS = 3
SRC = 4
AXES = ("fibre", "seg")
LANES = 128
STEP = 32
HALO = 16
ROWS = PANELS * SRC
HALF_ROWS = ROWS // 2
VMEM = pl.BlockSpec(memory_space=pltpu.VMEM)
HBM = pl.BlockSpec(memory_space=pltpu.HBM)
SMALL = pltpu.CompilerParams(vmem_limit_bytes=16 * 2**20)
BF16 = jnp.bfloat16
F32 = jnp.float32


def split(x):
    high = x.astype(BF16)
    return high, (x - high.astype(F32)).astype(BF16)


def split_rows(x):
    high = x.astype(BF16).astype(F32)
    return jnp.concatenate([high, x - high, high], axis=0).astype(BF16)


def split_columns(x):
    high = x.astype(BF16).astype(F32)
    return jnp.concatenate([high, high, x - high], axis=1).astype(BF16)


def taps_at(taps_ref, index):
    total = jnp.zeros(index.shape, F32)
    for j in range(taps_ref.shape[0]):
        total = jnp.where(index == j, taps_ref[j], total)
    return total


def fir_matrix(fir_ref):
    lane = lax.broadcasted_iota(jnp.int32, (8, LANES), 1)
    row = lax.broadcasted_iota(jnp.int32, (8, LANES), 0)
    first = taps_at(fir_ref, lane - row)
    first = jnp.concatenate([first, jnp.zeros_like(first)], axis=1)
    return jnp.concatenate(
        [first if g == 0 else pltpu.roll(first, 8 * g, 1) for g in range(LANES // 8)], axis=0
    )


def to_blocks(x):
    return jnp.concatenate(
        [x[:, k : k + LANES] for k in range(0, x.shape[1], LANES)], axis=0
    )


def from_blocks(x, rows):
    return jnp.concatenate([x[k : k + rows] for k in range(0, x.shape[0], rows)], axis=1)


def earlier(x, rows):
    return jnp.concatenate([jnp.zeros((rows, x.shape[1]), x.dtype), x[:-rows]], axis=0)


def later(x, rows):
    return jnp.concatenate([x[rows:], jnp.zeros((rows, x.shape[1]), x.dtype)], axis=0)


def window_bands():
    u = lax.broadcasted_iota(jnp.int32, (2 * LANES, LANES), 0) % LANES
    t = lax.broadcasted_iota(jnp.int32, (2 * LANES, LANES), 1)
    bands = [jnp.abs(u - t) <= RUN, u - t >= LANES - RUN, t - u >= LANES - RUN]
    return jnp.concatenate([jnp.where(b, 1.0, 0.0).astype(BF16) for b in bands], axis=1)


def filter_and_norm(x, fir_both, fir_low, window):
    rows, samples = x.shape
    high, low = split(to_blocks(x))
    dot = functools.partial(jnp.dot, preferred_element_type=F32)
    full = dot(jnp.concatenate([high, low], axis=1), fir_both) + dot(high, fir_low)
    smooth = full[:, :LANES] + earlier(full[:, LANES:], rows)
    high, low = split(jnp.abs(smooth))
    sums = dot(jnp.concatenate([high, low], axis=1), window)
    total = (
        sums[:, :LANES]
        + earlier(sums[:, LANES : 2 * LANES], rows)
        + later(sums[:, 2 * LANES :], rows)
    )
    shape = total.shape
    where = lax.broadcasted_iota(jnp.int32, shape, 0) // rows * LANES
    where = where + lax.broadcasted_iota(jnp.int32, shape, 1)
    count = jnp.minimum(where, RUN) + jnp.minimum(samples - 1 - where, RUN) + 1
    level = total / count.astype(F32)
    return from_blocks(smooth / (level + 1e-5), rows)


def pack(x):
    width = x.shape[1] // 4
    tail = x[:, 3 * width :]
    more = [
        jnp.concatenate([tail[k : k + 1] for k in range(3 * g, 3 * g + 3)], axis=1)
        for g in range(2)
    ]
    return jnp.concatenate([x[:, : 3 * width]] + more, axis=0)


def unpack(x):
    width = x.shape[1] // 3
    tail = [x[6 + k // 3 : 7 + k // 3, k % 3 * width : (k % 3 + 1) * width] for k in range(6)]
    return jnp.concatenate([x[:6], jnp.concatenate(tail, axis=0)], axis=1)


def parity(number):
    total = 0
    for k in range(16):
        total = total ^ (number >> k)
    return total & 1


def fetch(pairs, sems):
    copies = [pltpu.make_async_copy(a, b, sems.at[i]) for i, (a, b) in enumerate(pairs)]
    for copy in copies:
        copy.start()
    return copies


def load_kernel(
    strain_hbm,
    space_hbm,
    sources_hbm,
    near_ref,
    outer_ref,
    part_ref,
    matrix_ref,
    space_ref,
    sources_ref,
    sems,
):
    copies = fetch(
        [(sources_hbm, sources_ref), (space_hbm, space_ref), (strain_hbm, near_ref)], sems
    )
    channels = near_ref.shape[0]
    me = lax.axis_index(AXES)
    half = parity(me)
    half_span = (space_ref.shape[0] - 1) // 2
    copies[0].wait()
    shape = (16, 2 * channels)
    row = lax.broadcasted_iota(jnp.int32, shape, 0)
    lane = lax.broadcasted_iota(jnp.int32, shape, 1)
    source = jnp.full(shape, -(1 << 20), jnp.int32)
    for k in range(HALF_ROWS):
        number = half * HALF_ROWS + k
        source = jnp.where(row == k, sources_ref[number // SRC, number % SRC], source)
    copies[1].wait()
    matrix = taps_at(space_ref, lane + (me - me % 2) * channels - source + half_span)
    even = me % 2 == 0
    own = jnp.where(even, matrix[:, :channels], matrix[:, channels:])
    other = jnp.where(even, matrix[:, channels:], matrix[:, :channels])
    matrix_ref[...] = split_columns(other)
    copies[2].wait()
    x = near_ref[...]
    outer_ref[...] = jnp.where(even, x[:HALO], x[channels - HALO :])
    part = jnp.dot(split_columns(own), split_rows(x), preferred_element_type=F32)
    part_ref[...] = pack(part[:HALF_ROWS])


def share_kernel(other_ref, part_ref, matrix_ref, total_ref):
    part = jnp.dot(matrix_ref[...], split_rows(other_ref[...]), preferred_element_type=F32)
    total_ref[...] = part_ref[...] + pack(part[:HALF_ROWS])


def tables_kernel(
    fir_hbm, space_hbm, space_matrix_ref, both_ref, low_ref, window_ref, fir_ref, space_ref, sems
):
    copies = fetch([(space_hbm, space_ref), (fir_hbm, fir_ref)], sems)
    window_ref[...] = window_bands()
    channels = space_matrix_ref.shape[0]
    half_span = (space_ref.shape[0] - 1) // 2
    row = lax.broadcasted_iota(jnp.int32, (channels, channels + 2 * HALO), 0)
    column = lax.broadcasted_iota(jnp.int32, (channels, channels + 2 * HALO), 1)
    copies[0].wait()
    space_matrix_ref[...] = split_columns(taps_at(space_ref, column - HALO - row + half_span))
    copies[1].wait()
    high, low = split(fir_matrix(fir_ref))
    both_ref[...] = jnp.concatenate([high, high], axis=0)
    low_ref[...] = low


def channels_kernel(
    strain_ref,
    other_ref,
    outer_ref,
    space_matrix_ref,
    both_ref,
    low_ref,
    window_ref,
    shifted_ref,
):
    channels, samples = strain_ref.shape
    me = lax.axis_index(AXES)
    even = me % 2 == 0
    other, outer = other_ref[...], outer_ref[...]
    outer = jnp.where((me == 0) | (me == lax.axis_size(AXES) - 1), 0.0, outer)
    before = jnp.where(even, outer, other[channels - HALO :])
    after = jnp.where(even, other[:HALO], outer)
    x = jnp.concatenate([before, strain_ref[...], after], axis=0)
    spaced = jnp.dot(space_matrix_ref[...], split_rows(x), preferred_element_type=F32)
    normed = filter_and_norm(spaced, both_ref[...], low_ref[...], window_ref[...])
    length = shifted_ref.shape[1]
    padded = jnp.concatenate(
        [
            jnp.zeros((channels, LANES), F32),
            normed,
            jnp.zeros((channels, 2 * LANES), F32),
        ],
        axis=1,
    )
    per_tile = LANES // STEP
    for q in range(0, per_tile, 2):
        turned = [
            padded if k == 0 else pltpu.roll(padded, padded.shape[1] - STEP * k, 1)
            for k in (q, q + 1)
        ]
        pair = jnp.concatenate(turned, axis=0).astype(BF16)
        for h in range(LAGS // LANES):
            at = (h * per_tile + q) * channels
            shifted_ref[at : at + 2 * channels, :] = pair[:, h * LANES : h * LANES + length]


def swap(upper, lower, distance, lane):
    near = (lane // distance) % 2 == 0
    return (
        jnp.where(near, upper, pltpu.roll(lower, distance, 1)),
        jnp.where(near, pltpu.roll(upper, LANES - distance, 1), lower),
    )


def lag_sums(shifted_ref, normed):
    rows = HALF_ROWS
    samples = normed.shape[1]
    coarse = LAGS // STEP
    channels = shifted_ref.shape[0] // coarse
    padded = jnp.concatenate([normed, jnp.zeros((normed.shape[0], LANES), F32)], axis=1)
    lane = lax.broadcasted_iota(jnp.int32, (STEP, LANES), 1)
    row = lax.broadcasted_iota(jnp.int32, (STEP, LANES), 0)
    straight = lane >= row
    records = []
    for k in range(rows):
        one = jnp.broadcast_to(padded[k : k + 1], (STEP, padded.shape[1]))
        tiles = [
            pltpu.roll(one[:, j : j + LANES], 0, 1, stride=1, stride_axis=0)
            for j in range(0, padded.shape[1], LANES)
        ]
        previous = [tiles[-1]] + tiles[:-1]
        records.append(
            jnp.concatenate(
                [jnp.where(straight, b, a) for a, b in zip(previous, tiles)], axis=1
            ).astype(BF16)
        )
    records = jnp.concatenate(records, axis=0)
    result = lax.dot_general(
        shifted_ref[...], records, (((1,), (1,)), ((), ())), preferred_element_type=F32
    )
    result = result * float(samples) ** -0.5
    per_tile = LANES // STEP
    tiles = -(-rows // per_tile)
    short = tiles * LANES - result.shape[1]
    if short:
        result = jnp.concatenate([result, jnp.zeros((result.shape[0], short), F32)], axis=1)
    lane = lax.broadcasted_iota(jnp.int32, (channels, LANES), 1)
    sums = [[None] * (LAGS // LANES) for _ in range(rows)]
    for h in range(LAGS // LANES):
        for tile in range(tiles):
            parts = [
                result[
                    (h * per_tile + q) * channels : (h * per_tile + q + 1) * channels,
                    tile * LANES : (tile + 1) * LANES,
                ]
                for q in range(per_tile)
            ]
            for distance in [d for d in (8, 4, 2, 1) if d < per_tile]:
                for q in range(per_tile):
                    if q & distance == 0:
                        parts[q], parts[q + distance] = swap(
                            parts[q], parts[q + distance], distance * STEP, lane
                        )
            for q in range(per_tile):
                if tile * per_tile + q < rows:
                    sums[tile * per_tile + q][h] = parts[q]
    return sums


def norm_kernel(total_ref, both_ref, low_ref, window_ref, normed_ref):
    spaced = unpack(total_ref[...])
    samples = spaced.shape[1]
    spaced = jnp.concatenate([spaced, jnp.zeros((8 - HALF_ROWS, samples), F32)], axis=0)
    normed = filter_and_norm(spaced, both_ref[...], low_ref[...], window_ref[...])
    normed = jnp.concatenate([normed[:, : samples // 2], normed[:, samples // 2 :]], axis=0)
    normed_ref[...] = normed.astype(BF16)


def rows_of(normed_ref):
    x = normed_ref[...].astype(F32)
    return jnp.concatenate([x[:8], x[8:]], axis=1)


def first_kernel(normed_ref, shifted_ref, sums_ref):
    for k, halves in enumerate(lag_sums(shifted_ref, rows_of(normed_ref))):
        for h, part in enumerate(halves):
            sums_ref[k, :, h * LANES : (h + 1) * LANES] = part


def second_kernel(normed_ref, shifted_ref, sums_ref, out_hbm, more_ref, sems):
    mine = parity(lax.axis_index(AXES))
    early = pltpu.make_async_copy(
        sums_ref, out_hbm.at[pl.ds(mine * HALF_ROWS, HALF_ROWS)], sems.at[0]
    )
    early.start()
    for k, halves in enumerate(lag_sums(shifted_ref, rows_of(normed_ref))):
        for h, part in enumerate(halves):
            more_ref[k, :, h * LANES : (h + 1) * LANES] = part
    late = pltpu.make_async_copy(
        more_ref, out_hbm.at[pl.ds((1 - mine) * HALF_ROWS, HALF_ROWS)], sems.at[1]
    )
    late.start()
    early.wait()
    late.wait()


def in_hbm(x):
    return pltpu.with_memory_space_constraint(x, pltpu.HBM)


def local(strain, fir_taps, space_taps, sources):
    channels, samples = strain.shape
    devices = lax.axis_size(AXES)

    def partner(x, mask):
        return lax.ppermute(x, AXES, [(i, i ^ mask) for i in range(devices)])

    beside = partner(strain, 1)
    packed = jax.ShapeDtypeStruct((8, samples * 3 // 4), F32)
    near, outer, part, matrix = pl.pallas_call(
        load_kernel,
        out_shape=[
            jax.ShapeDtypeStruct(strain.shape, F32),
            jax.ShapeDtypeStruct((HALO, samples), F32),
            packed,
            jax.ShapeDtypeStruct((16, 3 * channels), BF16),
        ],
        in_specs=[HBM] * 3,
        out_specs=[VMEM] * 4,
        scratch_shapes=[
            pltpu.SMEM(space_taps.shape, F32),
            pltpu.SMEM(sources.shape, jnp.int32),
            pltpu.SemaphoreType.DMA((3,)),
        ],
        compiler_params=SMALL,
        name="load",
    )(*[in_hbm(x) for x in (strain, space_taps, sources)])
    total = pl.pallas_call(
        share_kernel,
        out_shape=packed,
        in_specs=[VMEM] * 3,
        out_specs=VMEM,
        compiler_params=SMALL,
        name="share",
    )(beside, part, matrix)
    across = [(0, 2), (2, 1), (1, 0)]
    across += [(devices - 1, devices - 3), (devices - 3, devices - 2), (devices - 2, devices - 1)]
    for k in range(3, devices - 4, 2):
        across += [(k, k + 1), (k + 1, k)]
    me = lax.axis_index(AXES)
    outer = jnp.where(me == 0, beside[channels - HALO :], outer)
    outer = jnp.where(me == devices - 1, beside[:HALO], outer)
    steps = [1 << k for k in range(1, devices.bit_length() - 1)]
    order = [(distance + 1,) for distance in steps[:1:-1]] + [(5, 3, 6)]
    for place, masks in enumerate(order):
        if place == 0:
            total, outer = lax.optimization_barrier((total, outer))
            outer = lax.ppermute(outer, AXES, across)
        if place == 1:
            total, fir_taps, space_taps = lax.optimization_barrier((total, fir_taps, space_taps))
            tables = pl.pallas_call(
                tables_kernel,
                out_shape=[
                    jax.ShapeDtypeStruct((channels, 3 * (channels + 2 * HALO)), BF16),
                    jax.ShapeDtypeStruct((2 * LANES, 2 * LANES), BF16),
                    jax.ShapeDtypeStruct((LANES, 2 * LANES), BF16),
                    jax.ShapeDtypeStruct((2 * LANES, 3 * LANES), BF16),
                ],
                in_specs=[HBM] * 2,
                out_specs=[VMEM] * 4,
                scratch_shapes=[
                    pltpu.SMEM(fir_taps.shape, F32),
                    pltpu.SMEM(space_taps.shape, F32),
                    pltpu.SemaphoreType.DMA((2,)),
                ],
                compiler_params=SMALL,
                name="tables",
            )(in_hbm(fir_taps), in_hbm(space_taps))
        if place == len(order) - 1:
            total, *tables = lax.optimization_barrier((total, *tables))
            shifted = pl.pallas_call(
                channels_kernel,
                out_shape=jax.ShapeDtypeStruct(
                    (LAGS // STEP * channels, samples + LANES), BF16
                ),
                in_specs=[VMEM] * 7,
                out_specs=VMEM,
                compiler_params=SMALL,
                name="channels",
            )(near, beside, outer, *tables)
        total = sum([partner(total, mask) for mask in masks], total)
    total, shifted = lax.optimization_barrier((total, shifted))
    mine = pl.pallas_call(
        norm_kernel,
        out_shape=jax.ShapeDtypeStruct((16, samples // 2), BF16),
        in_specs=[VMEM] * 4,
        out_specs=VMEM,
        compiler_params=SMALL,
        name="norm",
    )(total, *tables[1:])
    other = partner(mine, 1)
    sums = jax.ShapeDtypeStruct((HALF_ROWS, channels, LAGS), F32)
    first = pl.pallas_call(
        first_kernel,
        out_shape=sums,
        in_specs=[VMEM] * 2,
        out_specs=VMEM,
        compiler_params=SMALL,
        name="first",
    )(mine, shifted)
    out = pl.pallas_call(
        second_kernel,
        out_shape=jax.ShapeDtypeStruct((ROWS, channels, LAGS), F32),
        in_specs=[VMEM] * 3,
        out_specs=HBM,
        scratch_shapes=[pltpu.VMEM(sums.shape, F32), pltpu.SemaphoreType.DMA((2,))],
        compiler_params=SMALL,
        name="second",
    )(other, shifted, first)
    return out.reshape(PANELS, SRC, channels, LAGS)


def solution(mesh):
    return jax.shard_map(
        local,
        mesh=mesh,
        in_specs=(P(AXES, None), P(), P(), P()),
        out_specs=P(None, None, AXES, None),
        check_vma=False,
    )
```

```python
import functools

import jax
import jax.numpy as jnp
from jax import lax
from jax.experimental import pallas as pl
from jax.experimental.pallas import tpu as pltpu
from jax.sharding import PartitionSpec as P

RUN = 64
LAGS = 256
PANELS = 3
SRC = 4
AXES = ("fibre", "seg")
LANES = 128
STEP = 32
HALO = 16
ROWS = PANELS * SRC
HALF_ROWS = ROWS // 2
VMEM = pl.BlockSpec(memory_space=pltpu.VMEM)
HBM = pl.BlockSpec(memory_space=pltpu.HBM)
SMALL = pltpu.CompilerParams(vmem_limit_bytes=16 * 2**20)
BF16 = jnp.bfloat16
F32 = jnp.float32


def split(x):
    high = x.astype(BF16)
    return high, (x - high.astype(F32)).astype(BF16)


def thirds(x):
    high = x.astype(BF16).astype(F32)
    rest = x - high
    middle = rest.astype(BF16).astype(F32)
    return high, middle, rest - middle


def data_terms(x, axis):
    high, middle, low = thirds(x)
    return jnp.concatenate([high, high, middle, high, low, middle], axis=axis).astype(BF16)


def tap_terms(x, axis):
    high, middle, low = thirds(x)
    return jnp.concatenate([high, middle, high, low, high, middle], axis=axis).astype(BF16)


def taps_at(taps_ref, index):
    total = jnp.zeros(index.shape, F32)
    for j in range(taps_ref.shape[0]):
        total = jnp.where(index == j, taps_ref[j], total)
    return total


def fir_matrix(fir_ref):
    lane = lax.broadcasted_iota(jnp.int32, (8, LANES), 1)
    row = lax.broadcasted_iota(jnp.int32, (8, LANES), 0)
    first = taps_at(fir_ref, lane - row)
    first = jnp.concatenate([first, jnp.zeros_like(first)], axis=1)
    return jnp.concatenate(
        [first if g == 0 else pltpu.roll(first, 8 * g, 1) for g in range(LANES // 8)], axis=0
    )


def to_blocks(x):
    return jnp.concatenate(
        [x[:, k : k + LANES] for k in range(0, x.shape[1], LANES)], axis=0
    )


def from_blocks(x, rows):
    return jnp.concatenate([x[k : k + rows] for k in range(0, x.shape[0], rows)], axis=1)


def earlier(x, rows):
    return jnp.concatenate([jnp.zeros((rows, x.shape[1]), x.dtype), x[:-rows]], axis=0)


def later(x, rows):
    return jnp.concatenate([x[rows:], jnp.zeros((rows, x.shape[1]), x.dtype)], axis=0)


def window_bands():
    u = lax.broadcasted_iota(jnp.int32, (2 * LANES, LANES), 0) % LANES
    t = lax.broadcasted_iota(jnp.int32, (2 * LANES, LANES), 1)
    bands = [jnp.abs(u - t) <= RUN, u - t >= LANES - RUN, t - u >= LANES - RUN]
    return jnp.concatenate([jnp.where(b, 1.0, 0.0).astype(BF16) for b in bands], axis=1)


def filter_and_norm(x, fir_terms, window):
    rows, samples = x.shape
    dot = functools.partial(jnp.dot, preferred_element_type=F32)
    full = dot(data_terms(to_blocks(x), 1), fir_terms)
    smooth = full[:, :LANES] + earlier(full[:, LANES:], rows)
    high, low = split(jnp.abs(smooth))
    sums = dot(jnp.concatenate([high, low], axis=1), window)
    total = (
        sums[:, :LANES]
        + earlier(sums[:, LANES : 2 * LANES], rows)
        + later(sums[:, 2 * LANES :], rows)
    )
    shape = total.shape
    where = lax.broadcasted_iota(jnp.int32, shape, 0) // rows * LANES
    where = where + lax.broadcasted_iota(jnp.int32, shape, 1)
    count = jnp.minimum(where, RUN) + jnp.minimum(samples - 1 - where, RUN) + 1
    level = total / count.astype(F32)
    return from_blocks(smooth / (level + 1e-5), rows)


def pack(x):
    width = x.shape[1] // 4
    tail = x[:, 3 * width :]
    more = [
        jnp.concatenate([tail[k : k + 1] for k in range(3 * g, 3 * g + 3)], axis=1)
        for g in range(2)
    ]
    return jnp.concatenate([x[:, : 3 * width]] + more, axis=0)


def unpack(x):
    width = x.shape[1] // 3
    tail = [x[6 + k // 3 : 7 + k // 3, k % 3 * width : (k % 3 + 1) * width] for k in range(6)]
    return jnp.concatenate([x[:6], jnp.concatenate(tail, axis=0)], axis=1)


def parity(number):
    total = 0
    for k in range(16):
        total = total ^ (number >> k)
    return total & 1


def fetch(pairs, sems):
    copies = [pltpu.make_async_copy(a, b, sems.at[i]) for i, (a, b) in enumerate(pairs)]
    for copy in copies:
        copy.start()
    return copies


def load_kernel(
    strain_hbm,
    space_hbm,
    sources_hbm,
    near_ref,
    outer_ref,
    part_ref,
    matrix_ref,
    space_ref,
    sources_ref,
    sems,
):
    copies = fetch(
        [(sources_hbm, sources_ref), (space_hbm, space_ref), (strain_hbm, near_ref)], sems
    )
    channels = near_ref.shape[0]
    me = lax.axis_index(AXES)
    half = parity(me)
    half_span = (space_ref.shape[0] - 1) // 2
    copies[0].wait()
    shape = (16, 2 * channels)
    row = lax.broadcasted_iota(jnp.int32, shape, 0)
    lane = lax.broadcasted_iota(jnp.int32, shape, 1)
    source = jnp.full(shape, -(1 << 20), jnp.int32)
    for k in range(HALF_ROWS):
        number = half * HALF_ROWS + k
        source = jnp.where(row == k, sources_ref[number // SRC, number % SRC], source)
    copies[1].wait()
    matrix = taps_at(space_ref, lane + (me - me % 2) * channels - source + half_span)
    even = me % 2 == 0
    own = jnp.where(even, matrix[:, :channels], matrix[:, channels:])
    other = jnp.where(even, matrix[:, channels:], matrix[:, :channels])
    matrix_ref[...] = tap_terms(other, 1)
    copies[2].wait()
    x = near_ref[...]
    outer_ref[...] = jnp.where(even, x[:HALO], x[channels - HALO :])
    part = jnp.dot(tap_terms(own, 1), data_terms(x, 0), preferred_element_type=F32)
    part_ref[...] = pack(part[:HALF_ROWS])


def share_kernel(other_ref, part_ref, matrix_ref, total_ref):
    part = jnp.dot(matrix_ref[...], data_terms(other_ref[...], 0), preferred_element_type=F32)
    total_ref[...] = part_ref[...] + pack(part[:HALF_ROWS])


def tables_kernel(
    fir_hbm, space_hbm, space_matrix_ref, fir_matrix_ref, window_ref, fir_ref, space_ref, sems
):
    copies = fetch([(space_hbm, space_ref), (fir_hbm, fir_ref)], sems)
    window_ref[...] = window_bands()
    channels = space_matrix_ref.shape[0]
    half_span = (space_ref.shape[0] - 1) // 2
    row = lax.broadcasted_iota(jnp.int32, (channels, channels + 2 * HALO), 0)
    column = lax.broadcasted_iota(jnp.int32, (channels, channels + 2 * HALO), 1)
    copies[0].wait()
    space_matrix_ref[...] = tap_terms(
        taps_at(space_ref, column - HALO - row + half_span), 1
    )
    copies[1].wait()
    fir_matrix_ref[...] = tap_terms(fir_matrix(fir_ref), 0)


def channels_kernel(
    strain_ref,
    other_ref,
    outer_ref,
    space_matrix_ref,
    fir_matrix_ref,
    window_ref,
    shifted_ref,
):
    channels, samples = strain_ref.shape
    me = lax.axis_index(AXES)
    even = me % 2 == 0
    other, outer = other_ref[...], outer_ref[...]
    outer = jnp.where((me == 0) | (me == lax.axis_size(AXES) - 1), 0.0, outer)
    before = jnp.where(even, outer, other[channels - HALO :])
    after = jnp.where(even, other[:HALO], outer)
    x = jnp.concatenate([before, strain_ref[...], after], axis=0)
    spaced = jnp.dot(space_matrix_ref[...], data_terms(x, 0), preferred_element_type=F32)
    normed = filter_and_norm(spaced, fir_matrix_ref[...], window_ref[...])
    length = shifted_ref.shape[1]
    padded = jnp.concatenate(
        [
            jnp.zeros((channels, LANES), F32),
            normed,
            jnp.zeros((channels, 2 * LANES), F32),
        ],
        axis=1,
    )
    per_tile = LANES // STEP
    for q in range(0, per_tile, 2):
        turned = [
            padded if k == 0 else pltpu.roll(padded, padded.shape[1] - STEP * k, 1)
            for k in (q, q + 1)
        ]
        pair = jnp.concatenate(turned, axis=0).astype(BF16)
        for h in range(LAGS // LANES):
            at = (h * per_tile + q) * channels
            shifted_ref[at : at + 2 * channels, :] = pair[:, h * LANES : h * LANES + length]


def swap(upper, lower, distance, lane):
    near = (lane // distance) % 2 == 0
    return (
        jnp.where(near, upper, pltpu.roll(lower, distance, 1)),
        jnp.where(near, pltpu.roll(upper, LANES - distance, 1), lower),
    )


def lag_sums(shifted_ref, normed):
    rows = HALF_ROWS
    samples = normed.shape[1]
    coarse = LAGS // STEP
    channels = shifted_ref.shape[0] // coarse
    padded = jnp.concatenate([normed, jnp.zeros((normed.shape[0], LANES), F32)], axis=1)
    lane = lax.broadcasted_iota(jnp.int32, (STEP, LANES), 1)
    row = lax.broadcasted_iota(jnp.int32, (STEP, LANES), 0)
    straight = lane >= row
    records = []
    for k in range(rows):
        one = jnp.broadcast_to(padded[k : k + 1], (STEP, padded.shape[1]))
        tiles = [
            pltpu.roll(one[:, j : j + LANES], 0, 1, stride=1, stride_axis=0)
            for j in range(0, padded.shape[1], LANES)
        ]
        previous = [tiles[-1]] + tiles[:-1]
        records.append(
            jnp.concatenate(
                [jnp.where(straight, b, a) for a, b in zip(previous, tiles)], axis=1
            ).astype(BF16)
        )
    records = jnp.concatenate(records, axis=0)
    result = lax.dot_general(
        shifted_ref[...], records, (((1,), (1,)), ((), ())), preferred_element_type=F32
    )
    result = result * float(samples) ** -0.5
    per_tile = LANES // STEP
    tiles = -(-rows // per_tile)
    short = tiles * LANES - result.shape[1]
    if short:
        result = jnp.concatenate([result, jnp.zeros((result.shape[0], short), F32)], axis=1)
    lane = lax.broadcasted_iota(jnp.int32, (channels, LANES), 1)
    sums = [[None] * (LAGS // LANES) for _ in range(rows)]
    for h in range(LAGS // LANES):
        for tile in range(tiles):
            parts = [
                result[
                    (h * per_tile + q) * channels : (h * per_tile + q + 1) * channels,
                    tile * LANES : (tile + 1) * LANES,
                ]
                for q in range(per_tile)
            ]
            for distance in [d for d in (8, 4, 2, 1) if d < per_tile]:
                for q in range(per_tile):
                    if q & distance == 0:
                        parts[q], parts[q + distance] = swap(
                            parts[q], parts[q + distance], distance * STEP, lane
                        )
            for q in range(per_tile):
                if tile * per_tile + q < rows:
                    sums[tile * per_tile + q][h] = parts[q]
    return sums


def norm_kernel(total_ref, fir_matrix_ref, window_ref, normed_ref):
    spaced = unpack(total_ref[...])
    samples = spaced.shape[1]
    spaced = jnp.concatenate([spaced, jnp.zeros((8 - HALF_ROWS, samples), F32)], axis=0)
    normed = filter_and_norm(spaced, fir_matrix_ref[...], window_ref[...])
    normed = jnp.concatenate([normed[:, : samples // 2], normed[:, samples // 2 :]], axis=0)
    normed_ref[...] = normed.astype(BF16)


def rows_of(normed_ref):
    x = normed_ref[...].astype(F32)
    return jnp.concatenate([x[:8], x[8:]], axis=1)


def first_kernel(normed_ref, shifted_ref, sums_ref):
    for k, halves in enumerate(lag_sums(shifted_ref, rows_of(normed_ref))):
        for h, part in enumerate(halves):
            sums_ref[k, :, h * LANES : (h + 1) * LANES] = part


def second_kernel(normed_ref, shifted_ref, sums_ref, out_hbm, more_ref, sems):
    mine = parity(lax.axis_index(AXES))
    early = pltpu.make_async_copy(
        sums_ref, out_hbm.at[pl.ds(mine * HALF_ROWS, HALF_ROWS)], sems.at[0]
    )
    early.start()
    for k, halves in enumerate(lag_sums(shifted_ref, rows_of(normed_ref))):
        for h, part in enumerate(halves):
            more_ref[k, :, h * LANES : (h + 1) * LANES] = part
    late = pltpu.make_async_copy(
        more_ref, out_hbm.at[pl.ds((1 - mine) * HALF_ROWS, HALF_ROWS)], sems.at[1]
    )
    late.start()
    early.wait()
    late.wait()


def in_hbm(x):
    return pltpu.with_memory_space_constraint(x, pltpu.HBM)


def local(strain, fir_taps, space_taps, sources):
    channels, samples = strain.shape
    devices = lax.axis_size(AXES)

    def partner(x, mask):
        return lax.ppermute(x, AXES, [(i, i ^ mask) for i in range(devices)])

    beside = partner(strain, 1)
    packed = jax.ShapeDtypeStruct((8, samples * 3 // 4), F32)
    near, outer, part, matrix = pl.pallas_call(
        load_kernel,
        out_shape=[
            jax.ShapeDtypeStruct(strain.shape, F32),
            jax.ShapeDtypeStruct((HALO, samples), F32),
            packed,
            jax.ShapeDtypeStruct((16, 6 * channels), BF16),
        ],
        in_specs=[HBM] * 3,
        out_specs=[VMEM] * 4,
        scratch_shapes=[
            pltpu.SMEM(space_taps.shape, F32),
            pltpu.SMEM(sources.shape, jnp.int32),
            pltpu.SemaphoreType.DMA((3,)),
        ],
        compiler_params=SMALL,
        name="load",
    )(*[in_hbm(x) for x in (strain, space_taps, sources)])
    total = pl.pallas_call(
        share_kernel,
        out_shape=packed,
        in_specs=[VMEM] * 3,
        out_specs=VMEM,
        compiler_params=SMALL,
        name="share",
    )(beside, part, matrix)
    across = [(0, 2), (2, 1), (1, 0)]
    across += [(devices - 1, devices - 3), (devices - 3, devices - 2), (devices - 2, devices - 1)]
    for k in range(3, devices - 4, 2):
        across += [(k, k + 1), (k + 1, k)]
    me = lax.axis_index(AXES)
    outer = jnp.where(me == 0, beside[channels - HALO :], outer)
    outer = jnp.where(me == devices - 1, beside[:HALO], outer)
    steps = [1 << k for k in range(1, devices.bit_length() - 1)]
    order = [(distance + 1,) for distance in steps[:1:-1]] + [(5, 3, 6)]
    for place, masks in enumerate(order):
        if place == 0:
            total, outer = lax.optimization_barrier((total, outer))
            outer = lax.ppermute(outer, AXES, across)
        if place == 1:
            total, fir_taps, space_taps = lax.optimization_barrier((total, fir_taps, space_taps))
            tables = pl.pallas_call(
                tables_kernel,
                out_shape=[
                    jax.ShapeDtypeStruct((channels, 6 * (channels + 2 * HALO)), BF16),
                    jax.ShapeDtypeStruct((6 * LANES, 2 * LANES), BF16),
                    jax.ShapeDtypeStruct((2 * LANES, 3 * LANES), BF16),
                ],
                in_specs=[HBM] * 2,
                out_specs=[VMEM] * 3,
                scratch_shapes=[
                    pltpu.SMEM(fir_taps.shape, F32),
                    pltpu.SMEM(space_taps.shape, F32),
                    pltpu.SemaphoreType.DMA((2,)),
                ],
                compiler_params=SMALL,
                name="tables",
            )(in_hbm(fir_taps), in_hbm(space_taps))
        if place == len(order) - 1:
            total, *tables = lax.optimization_barrier((total, *tables))
            shifted = pl.pallas_call(
                channels_kernel,
                out_shape=jax.ShapeDtypeStruct(
                    (LAGS // STEP * channels, samples + LANES), BF16
                ),
                in_specs=[VMEM] * 6,
                out_specs=VMEM,
                compiler_params=SMALL,
                name="channels",
            )(near, beside, outer, *tables)
        total = sum([partner(total, mask) for mask in masks], total)
    total, shifted = lax.optimization_barrier((total, shifted))
    mine = pl.pallas_call(
        norm_kernel,
        out_shape=jax.ShapeDtypeStruct((16, samples // 2), BF16),
        in_specs=[VMEM] * 3,
        out_specs=VMEM,
        compiler_params=SMALL,
        name="norm",
    )(total, *tables[1:])
    other = partner(mine, 1)
    sums = jax.ShapeDtypeStruct((HALF_ROWS, channels, LAGS), F32)
    first = pl.pallas_call(
        first_kernel,
        out_shape=sums,
        in_specs=[VMEM] * 2,
        out_specs=VMEM,
        compiler_params=SMALL,
        name="first",
    )(mine, shifted)
    out = pl.pallas_call(
        second_kernel,
        out_shape=jax.ShapeDtypeStruct((ROWS, channels, LAGS), F32),
        in_specs=[VMEM] * 3,
        out_specs=HBM,
        scratch_shapes=[pltpu.VMEM(sums.shape, F32), pltpu.SemaphoreType.DMA((2,))],
        compiler_params=SMALL,
        name="second",
    )(other, shifted, first)
    return out.reshape(PANELS, SRC, channels, LAGS)


def solution(mesh):
    return jax.shard_map(
        local,
        mesh=mesh,
        in_specs=(P(AXES, None), P(), P(), P()),
        out_specs=P(None, None, AXES, None),
        check_vma=False,
    )
```

```python
import functools

import jax
import jax.numpy as jnp
from jax import lax
from jax.experimental import pallas as pl
from jax.experimental.pallas import tpu as pltpu
from jax.sharding import PartitionSpec as P

RUN = 64
LAGS = 256
PANELS = 3
SRC = 4
AXES = ("fibre", "seg")
LANES = 128
STEP = 32
HALO = 16
ROWS = PANELS * SRC
HALF_ROWS = ROWS // 2
VMEM = pl.BlockSpec(memory_space=pltpu.VMEM)
HBM = pl.BlockSpec(memory_space=pltpu.HBM)
SMALL = pltpu.CompilerParams(vmem_limit_bytes=16 * 2**20)
BF16 = jnp.bfloat16
F32 = jnp.float32


def split(x):
    high = x.astype(BF16)
    return high, (x - high.astype(F32)).astype(BF16)


def thirds(x):
    high = x.astype(BF16).astype(F32)
    rest = x - high
    middle = rest.astype(BF16).astype(F32)
    return high, middle, rest - middle


def data_terms(x, axis):
    high, middle, low = thirds(x)
    return jnp.concatenate([high, high, middle, high, low, middle], axis=axis).astype(BF16)


def tap_terms(x, axis):
    high, middle, low = thirds(x)
    return jnp.concatenate([high, middle, high, low, high, middle], axis=axis).astype(BF16)


def taps_at(taps_ref, index):
    total = jnp.zeros(index.shape, F32)
    for j in range(taps_ref.shape[0]):
        total = jnp.where(index == j, taps_ref[j], total)
    return total


def fir_matrix(fir_ref):
    lane = lax.broadcasted_iota(jnp.int32, (8, LANES), 1)
    row = lax.broadcasted_iota(jnp.int32, (8, LANES), 0)
    first = taps_at(fir_ref, lane - row)
    first = jnp.concatenate([first, jnp.zeros_like(first)], axis=1)
    return jnp.concatenate(
        [first if g == 0 else pltpu.roll(first, 8 * g, 1) for g in range(LANES // 8)], axis=0
    )


def to_blocks(x):
    return jnp.concatenate(
        [x[:, k : k + LANES] for k in range(0, x.shape[1], LANES)], axis=0
    )


def from_blocks(x, rows):
    return jnp.concatenate([x[k : k + rows] for k in range(0, x.shape[0], rows)], axis=1)


def earlier(x, rows):
    return jnp.concatenate([jnp.zeros((rows, x.shape[1]), x.dtype), x[:-rows]], axis=0)


def later(x, rows):
    return jnp.concatenate([x[rows:], jnp.zeros((rows, x.shape[1]), x.dtype)], axis=0)


def window_bands():
    u = lax.broadcasted_iota(jnp.int32, (2 * LANES, LANES), 0) % LANES
    t = lax.broadcasted_iota(jnp.int32, (2 * LANES, LANES), 1)
    bands = [jnp.abs(u - t) <= RUN, u - t >= LANES - RUN, t - u >= LANES - RUN]
    return jnp.concatenate([jnp.where(b, 1.0, 0.0).astype(BF16) for b in bands], axis=1)


def filter_and_norm(x, fir_terms, window):
    rows, samples = x.shape
    dot = functools.partial(jnp.dot, preferred_element_type=F32)
    full = dot(data_terms(to_blocks(x), 1), fir_terms)
    smooth = full[:, :LANES] + earlier(full[:, LANES:], rows)
    high, low = split(jnp.abs(smooth))
    sums = dot(jnp.concatenate([high, low], axis=1), window)
    total = (
        sums[:, :LANES]
        + earlier(sums[:, LANES : 2 * LANES], rows)
        + later(sums[:, 2 * LANES :], rows)
    )
    shape = total.shape
    where = lax.broadcasted_iota(jnp.int32, shape, 0) // rows * LANES
    where = where + lax.broadcasted_iota(jnp.int32, shape, 1)
    count = jnp.minimum(where, RUN) + jnp.minimum(samples - 1 - where, RUN) + 1
    level = total / count.astype(F32)
    return from_blocks(smooth / (level + 1e-5), rows)


def pack(x):
    width = x.shape[1] // 4
    tail = x[:, 3 * width :]
    more = [
        jnp.concatenate([tail[k : k + 1] for k in range(3 * g, 3 * g + 3)], axis=1)
        for g in range(2)
    ]
    return jnp.concatenate([x[:, : 3 * width]] + more, axis=0)


def unpack(x):
    width = x.shape[1] // 3
    tail = [x[6 + k // 3 : 7 + k // 3, k % 3 * width : (k % 3 + 1) * width] for k in range(6)]
    return jnp.concatenate([x[:6], jnp.concatenate(tail, axis=0)], axis=1)


def parity(number):
    total = 0
    for k in range(16):
        total = total ^ (number >> k)
    return total & 1


def fetch(pairs, sems):
    copies = [pltpu.make_async_copy(a, b, sems.at[i]) for i, (a, b) in enumerate(pairs)]
    for copy in copies:
        copy.start()
    return copies


def load_kernel(
    strain_hbm,
    space_hbm,
    sources_hbm,
    near_ref,
    outer_ref,
    part_ref,
    matrix_ref,
    space_ref,
    sources_ref,
    sems,
):
    copies = fetch(
        [(sources_hbm, sources_ref), (space_hbm, space_ref), (strain_hbm, near_ref)], sems
    )
    channels = near_ref.shape[0]
    me = lax.axis_index(AXES)
    half = parity(me)
    half_span = (space_ref.shape[0] - 1) // 2
    copies[0].wait()
    shape = (16, 2 * channels)
    row = lax.broadcasted_iota(jnp.int32, shape, 0)
    lane = lax.broadcasted_iota(jnp.int32, shape, 1)
    source = jnp.full(shape, -(1 << 20), jnp.int32)
    for k in range(HALF_ROWS):
        number = half * HALF_ROWS + k
        source = jnp.where(row == k, sources_ref[number // SRC, number % SRC], source)
    copies[1].wait()
    matrix = taps_at(space_ref, lane + (me - me % 2) * channels - source + half_span)
    even = me % 2 == 0
    own = jnp.where(even, matrix[:, :channels], matrix[:, channels:])
    other = jnp.where(even, matrix[:, channels:], matrix[:, :channels])
    matrix_ref[...] = tap_terms(other, 1)
    copies[2].wait()
    x = near_ref[...]
    outer_ref[...] = jnp.where(even, x[:HALO], x[channels - HALO :])
    part = jnp.dot(tap_terms(own, 1), data_terms(x, 0), preferred_element_type=F32)
    part_ref[...] = pack(part[:HALF_ROWS])


def share_kernel(other_ref, part_ref, matrix_ref, outer_ref, total_ref, sent_ref):
    del outer_ref
    me, channels = lax.axis_index(AXES), other_ref.shape[0]

    @pl.when(me == 0)
    def _():
        sent_ref[...] = other_ref[channels - HALO :, :]

    @pl.when(me == lax.axis_size(AXES) - 1)
    def _():
        sent_ref[...] = other_ref[:HALO, :]

    part = jnp.dot(matrix_ref[...], data_terms(other_ref[...], 0), preferred_element_type=F32)
    total_ref[...] = part_ref[...] + pack(part[:HALF_ROWS])


def tables_kernel(
    fir_hbm, space_hbm, space_matrix_ref, fir_matrix_ref, window_ref, fir_ref, space_ref, sems
):
    copies = fetch([(space_hbm, space_ref), (fir_hbm, fir_ref)], sems)
    window_ref[...] = window_bands()
    channels = space_matrix_ref.shape[0]
    half_span = (space_ref.shape[0] - 1) // 2
    row = lax.broadcasted_iota(jnp.int32, (channels, channels + 2 * HALO), 0)
    column = lax.broadcasted_iota(jnp.int32, (channels, channels + 2 * HALO), 1)
    copies[0].wait()
    space_matrix_ref[...] = tap_terms(
        taps_at(space_ref, column - HALO - row + half_span), 1
    )
    copies[1].wait()
    fir_matrix_ref[...] = tap_terms(fir_matrix(fir_ref), 0)


def channels_kernel(
    strain_ref,
    other_ref,
    outer_ref,
    space_matrix_ref,
    fir_matrix_ref,
    window_ref,
    shifted_ref,
):
    channels, samples = strain_ref.shape
    me = lax.axis_index(AXES)
    even = me % 2 == 0
    other, outer = other_ref[...], outer_ref[...]
    outer = jnp.where((me == 0) | (me == lax.axis_size(AXES) - 1), 0.0, outer)
    before = jnp.where(even, outer, other[channels - HALO :])
    after = jnp.where(even, other[:HALO], outer)
    x = jnp.concatenate([before, strain_ref[...], after], axis=0)
    spaced = jnp.dot(space_matrix_ref[...], data_terms(x, 0), preferred_element_type=F32)
    normed = filter_and_norm(spaced, fir_matrix_ref[...], window_ref[...])
    length = shifted_ref.shape[1]
    padded = jnp.concatenate(
        [
            jnp.zeros((channels, LANES), F32),
            normed,
            jnp.zeros((channels, 2 * LANES), F32),
        ],
        axis=1,
    )
    per_tile = LANES // STEP
    for q in range(0, per_tile, 2):
        turned = [
            padded if k == 0 else pltpu.roll(padded, padded.shape[1] - STEP * k, 1)
            for k in (q, q + 1)
        ]
        pair = jnp.concatenate(turned, axis=0).astype(BF16)
        for h in range(LAGS // LANES):
            at = (h * per_tile + q) * channels
            shifted_ref[at : at + 2 * channels, :] = pair[:, h * LANES : h * LANES + length]


def swap(upper, lower, distance, lane):
    near = (lane // distance) % 2 == 0
    return (
        jnp.where(near, upper, pltpu.roll(lower, distance, 1)),
        jnp.where(near, pltpu.roll(upper, LANES - distance, 1), lower),
    )


def lag_sums(shifted_ref, normed):
    rows = HALF_ROWS
    samples = normed.shape[1]
    coarse = LAGS // STEP
    channels = shifted_ref.shape[0] // coarse
    padded = jnp.concatenate([normed, jnp.zeros((normed.shape[0], LANES), F32)], axis=1)
    lane = lax.broadcasted_iota(jnp.int32, (STEP, LANES), 1)
    row = lax.broadcasted_iota(jnp.int32, (STEP, LANES), 0)
    straight = lane >= row
    records = []
    for k in range(rows):
        one = jnp.broadcast_to(padded[k : k + 1], (STEP, padded.shape[1]))
        tiles = [
            pltpu.roll(one[:, j : j + LANES], 0, 1, stride=1, stride_axis=0)
            for j in range(0, padded.shape[1], LANES)
        ]
        previous = [tiles[-1]] + tiles[:-1]
        records.append(
            jnp.concatenate(
                [jnp.where(straight, b, a) for a, b in zip(previous, tiles)], axis=1
            ).astype(BF16)
        )
    records = jnp.concatenate(records, axis=0)
    result = lax.dot_general(
        shifted_ref[...], records, (((1,), (1,)), ((), ())), preferred_element_type=F32
    )
    result = result * float(samples) ** -0.5
    per_tile = LANES // STEP
    tiles = -(-rows // per_tile)
    short = tiles * LANES - result.shape[1]
    if short:
        result = jnp.concatenate([result, jnp.zeros((result.shape[0], short), F32)], axis=1)
    lane = lax.broadcasted_iota(jnp.int32, (channels, LANES), 1)
    for tile in range(tiles):
        count = min(per_tile, rows - tile * per_tile)
        sums = [[] for _ in range(count)]
        for h in range(LAGS // LANES):
            parts = [
                result[
                    (h * per_tile + q) * channels : (h * per_tile + q + 1) * channels,
                    tile * LANES : (tile + 1) * LANES,
                ]
                for q in range(per_tile)
            ]
            for distance in [d for d in (8, 4, 2, 1) if d < per_tile]:
                for q in range(per_tile):
                    if q & distance == 0:
                        parts[q], parts[q + distance] = swap(
                            parts[q], parts[q + distance], distance * STEP, lane
                        )
            for q in range(count):
                sums[q].append(parts[q])
        yield tile * per_tile, [jnp.concatenate(halves, axis=1) for halves in sums]


def norm_kernel(*refs):
    *parts, fir_matrix_ref, window_ref, normed_ref = refs
    spaced = unpack(sum([ref[...] for ref in parts[1:]], parts[0][...]))
    samples = spaced.shape[1]
    spaced = jnp.concatenate([spaced, jnp.zeros((8 - HALF_ROWS, samples), F32)], axis=0)
    normed = filter_and_norm(spaced, fir_matrix_ref[...], window_ref[...])
    normed = jnp.concatenate([normed[:, : samples // 2], normed[:, samples // 2 :]], axis=0)
    normed_ref[...] = normed.astype(BF16)


def rows_of(normed_ref):
    x = normed_ref[...].astype(F32)
    return jnp.concatenate([x[:8], x[8:]], axis=1)


def first_kernel(normed_ref, shifted_ref, sums_ref):
    for start, group in lag_sums(shifted_ref, rows_of(normed_ref)):
        for k, sums in enumerate(group):
            sums_ref[start + k] = sums


def second_kernel(normed_ref, shifted_ref, sums_ref, out_hbm, more_ref, sems):
    mine = parity(lax.axis_index(AXES))
    early = pltpu.make_async_copy(
        sums_ref, out_hbm.at[pl.ds(mine * HALF_ROWS, HALF_ROWS)], sems.at[0]
    )
    early.start()
    copies = [early]
    for start, group in lag_sums(shifted_ref, rows_of(normed_ref)):
        for k, sums in enumerate(group):
            more_ref[start + k] = sums
        late = pltpu.make_async_copy(
            more_ref.at[pl.ds(start, len(group))],
            out_hbm.at[pl.ds((1 - mine) * HALF_ROWS + start, len(group))],
            sems.at[len(copies)],
        )
        late.start()
        copies.append(late)
    for copy in copies:
        copy.wait()


def in_hbm(x):
    return pltpu.with_memory_space_constraint(x, pltpu.HBM)


def local(strain, fir_taps, space_taps, sources):
    channels, samples = strain.shape
    devices = lax.axis_size(AXES)

    def partner(x, mask):
        return lax.ppermute(x, AXES, [(i, i ^ mask) for i in range(devices)])

    beside = partner(strain, 1)
    packed = jax.ShapeDtypeStruct((8, samples * 3 // 4), F32)
    near, outer, part, matrix = pl.pallas_call(
        load_kernel,
        out_shape=[
            jax.ShapeDtypeStruct(strain.shape, F32),
            jax.ShapeDtypeStruct((HALO, samples), F32),
            packed,
            jax.ShapeDtypeStruct((16, 6 * channels), BF16),
        ],
        in_specs=[HBM] * 3,
        out_specs=[VMEM] * 4,
        scratch_shapes=[
            pltpu.SMEM(space_taps.shape, F32),
            pltpu.SMEM(sources.shape, jnp.int32),
            pltpu.SemaphoreType.DMA((3,)),
        ],
        compiler_params=SMALL,
        name="load",
    )(*[in_hbm(x) for x in (strain, space_taps, sources)])
    total, outer = pl.pallas_call(
        share_kernel,
        out_shape=[packed, jax.ShapeDtypeStruct(outer.shape, F32)],
        in_specs=[VMEM] * 4,
        out_specs=[VMEM] * 2,
        input_output_aliases={3: 1},
        compiler_params=SMALL,
        name="share",
    )(beside, part, matrix, outer)
    across = [(0, 2), (2, 1), (1, 0)]
    across += [(devices - 1, devices - 3), (devices - 3, devices - 2), (devices - 2, devices - 1)]
    for k in range(3, devices - 4, 2):
        across += [(k, k + 1), (k + 1, k)]
    steps = [1 << k for k in range(1, devices.bit_length() - 1)]
    order = [(distance + 1,) for distance in steps[:1:-1]] + [(6, 3, 5)]
    for place, masks in enumerate(order):
        if place == 0:
            total, outer = lax.optimization_barrier((total, outer))
            outer = lax.ppermute(outer, AXES, across)
        if place == 1:
            total, fir_taps, space_taps = lax.optimization_barrier((total, fir_taps, space_taps))
            tables = pl.pallas_call(
                tables_kernel,
                out_shape=[
                    jax.ShapeDtypeStruct((channels, 6 * (channels + 2 * HALO)), BF16),
                    jax.ShapeDtypeStruct((6 * LANES, 2 * LANES), BF16),
                    jax.ShapeDtypeStruct((2 * LANES, 3 * LANES), BF16),
                ],
                in_specs=[HBM] * 2,
                out_specs=[VMEM] * 3,
                scratch_shapes=[
                    pltpu.SMEM(fir_taps.shape, F32),
                    pltpu.SMEM(space_taps.shape, F32),
                    pltpu.SemaphoreType.DMA((2,)),
                ],
                compiler_params=SMALL,
                name="tables",
            )(in_hbm(fir_taps), in_hbm(space_taps))
        if place == len(order) - 1:
            total, *tables = lax.optimization_barrier((total, *tables))
            shifted = pl.pallas_call(
                channels_kernel,
                out_shape=jax.ShapeDtypeStruct(
                    (LAGS // STEP * channels, samples + LANES), BF16
                ),
                in_specs=[VMEM] * 6,
                out_specs=VMEM,
                compiler_params=SMALL,
                name="channels",
            )(near, beside, outer, *tables)
        received = [partner(total, mask) for mask in masks]
        if place < len(order) - 1:
            total = sum(received, total)
    received, shifted = lax.optimization_barrier((received, shifted))
    mine = pl.pallas_call(
        norm_kernel,
        out_shape=jax.ShapeDtypeStruct((16, samples // 2), BF16),
        in_specs=[VMEM] * (3 + len(received)),
        out_specs=VMEM,
        compiler_params=SMALL,
        name="norm",
    )(total, *received, *tables[1:])
    other = partner(mine, 1)
    sums = jax.ShapeDtypeStruct((HALF_ROWS, channels, LAGS), F32)
    groups = -(-HALF_ROWS * STEP // LANES)
    first = pl.pallas_call(
        first_kernel,
        out_shape=sums,
        in_specs=[VMEM] * 2,
        out_specs=VMEM,
        compiler_params=SMALL,
        name="first",
    )(mine, shifted)
    out = pl.pallas_call(
        second_kernel,
        out_shape=jax.ShapeDtypeStruct((ROWS, channels, LAGS), F32),
        in_specs=[VMEM] * 3,
        out_specs=HBM,
        scratch_shapes=[pltpu.VMEM(sums.shape, F32), pltpu.SemaphoreType.DMA((1 + groups,))],
        compiler_params=SMALL,
        name="second",
    )(other, shifted, first)
    return out.reshape(PANELS, SRC, channels, LAGS)


def solution(mesh):
    return jax.shard_map(
        local,
        mesh=mesh,
        in_specs=(P(AXES, None), P(), P(), P()),
        out_specs=P(None, None, AXES, None),
        check_vma=False,
    )
```

```python
import functools

import jax
import jax.numpy as jnp
from jax import lax
from jax.experimental import pallas as pl
from jax.experimental.pallas import tpu as pltpu
from jax.sharding import PartitionSpec as P

RUN = 64
LAGS = 256
PANELS = 3
SRC = 4
AXES = ("fibre", "seg")
LANES = 128
STEP = 32
HALO = 16
ROWS = PANELS * SRC
HALF_ROWS = ROWS // 2
VMEM = pl.BlockSpec(memory_space=pltpu.VMEM)
HBM = pl.BlockSpec(memory_space=pltpu.HBM)
SMALL = pltpu.CompilerParams(vmem_limit_bytes=16 * 2**20)
BF16 = jnp.bfloat16
F32 = jnp.float32


def split(x):
    high = x.astype(BF16)
    return high, (x - high.astype(F32)).astype(BF16)


def thirds(x):
    high = x.astype(BF16).astype(F32)
    rest = x - high
    middle = rest.astype(BF16).astype(F32)
    return high, middle, rest - middle


def data_terms(x, axis):
    high, middle, low = thirds(x)
    return jnp.concatenate([high, high, middle, high, low, middle], axis=axis).astype(BF16)


def tap_terms(x, axis):
    high, middle, low = thirds(x)
    return jnp.concatenate([high, middle, high, low, high, middle], axis=axis).astype(BF16)


def taps_at(taps_ref, index):
    total = jnp.zeros(index.shape, F32)
    for j in range(taps_ref.shape[0]):
        total = jnp.where(index == j, taps_ref[j], total)
    return total


def fir_matrix(fir_ref):
    lane = lax.broadcasted_iota(jnp.int32, (8, LANES), 1)
    row = lax.broadcasted_iota(jnp.int32, (8, LANES), 0)
    first = taps_at(fir_ref, lane - row)
    first = jnp.concatenate([first, jnp.zeros_like(first)], axis=1)
    return jnp.concatenate(
        [first if g == 0 else pltpu.roll(first, 8 * g, 1) for g in range(LANES // 8)], axis=0
    )


def to_blocks(x):
    return jnp.concatenate(
        [x[:, k : k + LANES] for k in range(0, x.shape[1], LANES)], axis=0
    )


def from_blocks(x, rows):
    return jnp.concatenate([x[k : k + rows] for k in range(0, x.shape[0], rows)], axis=1)


def earlier(x, rows):
    return jnp.concatenate([jnp.zeros((rows, x.shape[1]), x.dtype), x[:-rows]], axis=0)


def later(x, rows):
    return jnp.concatenate([x[rows:], jnp.zeros((rows, x.shape[1]), x.dtype)], axis=0)


def window_bands():
    u = lax.broadcasted_iota(jnp.int32, (2 * LANES, LANES), 0) % LANES
    t = lax.broadcasted_iota(jnp.int32, (2 * LANES, LANES), 1)
    bands = [jnp.abs(u - t) <= RUN, u - t >= LANES - RUN, t - u >= LANES - RUN]
    return jnp.concatenate([jnp.where(b, 1.0, 0.0).astype(BF16) for b in bands], axis=1)


def filter_and_norm(x, fir_terms, window):
    rows, samples = x.shape
    dot = functools.partial(jnp.dot, preferred_element_type=F32)
    full = dot(data_terms(to_blocks(x), 1), fir_terms)
    smooth = full[:, :LANES] + earlier(full[:, LANES:], rows)
    high, low = split(jnp.abs(smooth))
    sums = dot(jnp.concatenate([high, low], axis=1), window)
    total = (
        sums[:, :LANES]
        + earlier(sums[:, LANES : 2 * LANES], rows)
        + later(sums[:, 2 * LANES :], rows)
    )
    shape = total.shape
    where = lax.broadcasted_iota(jnp.int32, shape, 0) // rows * LANES
    where = where + lax.broadcasted_iota(jnp.int32, shape, 1)
    count = jnp.minimum(where, RUN) + jnp.minimum(samples - 1 - where, RUN) + 1
    level = total / count.astype(F32)
    return from_blocks(smooth / (level + 1e-5), rows)


def pack(x):
    width = x.shape[1] // 4
    tail = x[:, 3 * width :]
    more = [
        jnp.concatenate([tail[k : k + 1] for k in range(3 * g, 3 * g + 3)], axis=1)
        for g in range(2)
    ]
    return jnp.concatenate([x[:, : 3 * width]] + more, axis=0)


def unpack(x):
    width = x.shape[1] // 3
    tail = [x[6 + k // 3 : 7 + k // 3, k % 3 * width : (k % 3 + 1) * width] for k in range(6)]
    return jnp.concatenate([x[:6], jnp.concatenate(tail, axis=0)], axis=1)


def parity(number):
    total = 0
    for k in range(16):
        total = total ^ (number >> k)
    return total & 1


def fetch(pairs, sems):
    copies = [pltpu.make_async_copy(a, b, sems.at[i]) for i, (a, b) in enumerate(pairs)]
    for copy in copies:
        copy.start()
    return copies


def load_kernel(
    strain_hbm,
    space_hbm,
    sources_hbm,
    near_ref,
    outer_ref,
    part_ref,
    matrix_ref,
    space_ref,
    sources_ref,
    sems,
):
    copies = fetch(
        [(sources_hbm, sources_ref), (space_hbm, space_ref), (strain_hbm, near_ref)], sems
    )
    channels = near_ref.shape[0]
    me = lax.axis_index(AXES)
    half = parity(me)
    half_span = (space_ref.shape[0] - 1) // 2
    copies[0].wait()
    shape = (16, 2 * channels)
    row = lax.broadcasted_iota(jnp.int32, shape, 0)
    lane = lax.broadcasted_iota(jnp.int32, shape, 1)
    source = jnp.full(shape, -(1 << 20), jnp.int32)
    for k in range(HALF_ROWS):
        number = half * HALF_ROWS + k
        source = jnp.where(row == k, sources_ref[number // SRC, number % SRC], source)
    copies[1].wait()
    matrix = taps_at(space_ref, lane + (me - me % 2) * channels - source + half_span)
    even = me % 2 == 0
    own = jnp.where(even, matrix[:, :channels], matrix[:, channels:])
    other = jnp.where(even, matrix[:, channels:], matrix[:, :channels])
    matrix_ref[...] = tap_terms(other, 1)
    copies[2].wait()
    x = near_ref[...]
    outer_ref[...] = jnp.where(even, x[:HALO], x[channels - HALO :])
    part = jnp.dot(tap_terms(own, 1), data_terms(x, 0), preferred_element_type=F32)
    part_ref[...] = pack(part[:HALF_ROWS])


def share_kernel(other_ref, part_ref, matrix_ref, outer_ref, total_ref, sent_ref):
    del outer_ref
    me, channels = lax.axis_index(AXES), other_ref.shape[0]

    @pl.when(me == 0)
    def _():
        sent_ref[...] = other_ref[channels - HALO :, :]

    @pl.when(me == lax.axis_size(AXES) - 1)
    def _():
        sent_ref[...] = other_ref[:HALO, :]

    part = jnp.dot(matrix_ref[...], data_terms(other_ref[...], 0), preferred_element_type=F32)
    total_ref[...] = part_ref[...] + pack(part[:HALF_ROWS])


def tables_kernel(
    fir_hbm, space_hbm, space_matrix_ref, fir_matrix_ref, window_ref, fir_ref, space_ref, sems
):
    copies = fetch([(space_hbm, space_ref), (fir_hbm, fir_ref)], sems)
    window_ref[...] = window_bands()
    channels = space_matrix_ref.shape[0]
    half_span = (space_ref.shape[0] - 1) // 2
    row = lax.broadcasted_iota(jnp.int32, (channels, channels + 2 * HALO), 0)
    column = lax.broadcasted_iota(jnp.int32, (channels, channels + 2 * HALO), 1)
    copies[0].wait()
    space_matrix_ref[...] = tap_terms(
        taps_at(space_ref, column - HALO - row + half_span), 1
    )
    copies[1].wait()
    fir_matrix_ref[...] = tap_terms(fir_matrix(fir_ref), 0)


def channels_kernel(
    strain_ref,
    other_ref,
    outer_ref,
    space_matrix_ref,
    fir_matrix_ref,
    window_ref,
    shifted_ref,
):
    channels, samples = strain_ref.shape
    me = lax.axis_index(AXES)
    even = me % 2 == 0
    other, outer = other_ref[...], outer_ref[...]
    outer = jnp.where((me == 0) | (me == lax.axis_size(AXES) - 1), 0.0, outer)
    before = jnp.where(even, outer, other[channels - HALO :])
    after = jnp.where(even, other[:HALO], outer)
    x = jnp.concatenate([before, strain_ref[...], after], axis=0)
    spaced = jnp.dot(space_matrix_ref[...], data_terms(x, 0), preferred_element_type=F32)
    normed = filter_and_norm(spaced, fir_matrix_ref[...], window_ref[...])
    length = shifted_ref.shape[1]
    padded = jnp.concatenate(
        [
            jnp.zeros((channels, LANES), F32),
            normed,
            jnp.zeros((channels, 2 * LANES), F32),
        ],
        axis=1,
    )
    per_tile = LANES // STEP
    for q in range(0, per_tile, 2):
        turned = [
            padded if k == 0 else pltpu.roll(padded, padded.shape[1] - STEP * k, 1)
            for k in (q, q + 1)
        ]
        pair = jnp.concatenate(turned, axis=0).astype(BF16)
        for h in range(LAGS // LANES):
            at = (h * per_tile + q) * channels
            shifted_ref[at : at + 2 * channels, :] = pair[:, h * LANES : h * LANES + length]


def swap(upper, lower, distance, lane):
    near = (lane // distance) % 2 == 0
    return (
        jnp.where(near, upper, pltpu.roll(lower, distance, 1)),
        jnp.where(near, pltpu.roll(upper, LANES - distance, 1), lower),
    )


def lag_sums(shifted_ref, normed):
    rows = HALF_ROWS
    samples = normed.shape[1]
    coarse = LAGS // STEP
    channels = shifted_ref.shape[0] // coarse
    padded = jnp.concatenate([normed, jnp.zeros((normed.shape[0], LANES), F32)], axis=1)
    lane = lax.broadcasted_iota(jnp.int32, (STEP, LANES), 1)
    row = lax.broadcasted_iota(jnp.int32, (STEP, LANES), 0)
    straight = lane >= row
    records = []
    for k in range(rows):
        one = jnp.broadcast_to(padded[k : k + 1], (STEP, padded.shape[1]))
        tiles = [
            pltpu.roll(one[:, j : j + LANES], 0, 1, stride=1, stride_axis=0)
            for j in range(0, padded.shape[1], LANES)
        ]
        previous = [tiles[-1]] + tiles[:-1]
        records.append(
            jnp.concatenate(
                [jnp.where(straight, b, a) for a, b in zip(previous, tiles)], axis=1
            ).astype(BF16)
        )
    records = jnp.concatenate(records, axis=0)
    result = lax.dot_general(
        shifted_ref[...], records, (((1,), (1,)), ((), ())), preferred_element_type=F32
    )
    result = result * float(samples) ** -0.5
    per_tile = LANES // STEP
    tiles = -(-rows // per_tile)
    short = tiles * LANES - result.shape[1]
    if short:
        result = jnp.concatenate([result, jnp.zeros((result.shape[0], short), F32)], axis=1)
    lane = lax.broadcasted_iota(jnp.int32, (channels, LANES), 1)
    for tile in range(tiles):
        count = min(per_tile, rows - tile * per_tile)
        sums = [[] for _ in range(count)]
        for h in range(LAGS // LANES):
            parts = [
                result[
                    (h * per_tile + q) * channels : (h * per_tile + q + 1) * channels,
                    tile * LANES : (tile + 1) * LANES,
                ]
                for q in range(per_tile)
            ]
            for distance in [d for d in (8, 4, 2, 1) if d < per_tile]:
                for q in range(per_tile):
                    if q & distance == 0:
                        parts[q], parts[q + distance] = swap(
                            parts[q], parts[q + distance], distance * STEP, lane
                        )
            for q in range(count):
                sums[q].append(parts[q])
        yield tile * per_tile, [jnp.concatenate(halves, axis=1) for halves in sums]


def norm_kernel(*refs):
    *parts, fir_matrix_ref, window_ref, normed_ref = refs
    spaced = unpack(sum([ref[...] for ref in parts[1:]], parts[0][...]))
    samples = spaced.shape[1]
    spaced = jnp.concatenate([spaced, jnp.zeros((8 - HALF_ROWS, samples), F32)], axis=0)
    normed = filter_and_norm(spaced, fir_matrix_ref[...], window_ref[...])
    normed = jnp.concatenate([normed[:, : samples // 2], normed[:, samples // 2 :]], axis=0)
    normed_ref[...] = normed.astype(BF16)


def rows_of(normed_ref):
    x = normed_ref[...].astype(F32)
    return jnp.concatenate([x[:8], x[8:]], axis=1)


def first_kernel(normed_ref, shifted_ref, sums_ref):
    for start, group in lag_sums(shifted_ref, rows_of(normed_ref)):
        for k, sums in enumerate(group):
            sums_ref[start + k] = sums


def second_kernel(normed_ref, shifted_ref, sums_ref, out_hbm, more_ref, sems):
    mine = parity(lax.axis_index(AXES))
    early = pltpu.make_async_copy(
        sums_ref, out_hbm.at[pl.ds(mine * HALF_ROWS, HALF_ROWS)], sems.at[0]
    )
    early.start()
    copies = [early]
    for start, group in lag_sums(shifted_ref, rows_of(normed_ref)):
        for k, sums in enumerate(group):
            more_ref[start + k] = sums
        late = pltpu.make_async_copy(
            more_ref.at[pl.ds(start, len(group))],
            out_hbm.at[pl.ds((1 - mine) * HALF_ROWS + start, len(group))],
            sems.at[len(copies)],
        )
        late.start()
        copies.append(late)
    for copy in copies:
        copy.wait()


def in_hbm(x):
    return pltpu.with_memory_space_constraint(x, pltpu.HBM)


def local(strain, fir_taps, space_taps, sources):
    channels, samples = strain.shape
    devices = lax.axis_size(AXES)

    def partner(x, mask):
        return lax.ppermute(x, AXES, [(i, i ^ mask) for i in range(devices)])

    beside = partner(strain, 1)
    packed = jax.ShapeDtypeStruct((8, samples * 3 // 4), F32)
    near, outer, part, matrix = pl.pallas_call(
        load_kernel,
        out_shape=[
            jax.ShapeDtypeStruct(strain.shape, F32),
            jax.ShapeDtypeStruct((HALO, samples), F32),
            packed,
            jax.ShapeDtypeStruct((16, 6 * channels), BF16),
        ],
        in_specs=[HBM] * 3,
        out_specs=[VMEM] * 4,
        scratch_shapes=[
            pltpu.SMEM(space_taps.shape, F32),
            pltpu.SMEM(sources.shape, jnp.int32),
            pltpu.SemaphoreType.DMA((3,)),
        ],
        compiler_params=SMALL,
        name="load",
    )(*[in_hbm(x) for x in (strain, space_taps, sources)])
    total, outer = pl.pallas_call(
        share_kernel,
        out_shape=[packed, jax.ShapeDtypeStruct(outer.shape, F32)],
        in_specs=[VMEM] * 4,
        out_specs=[VMEM] * 2,
        input_output_aliases={3: 1},
        compiler_params=SMALL,
        name="share",
    )(beside, part, matrix, outer)
    across = [(0, 2), (2, 1), (1, 0)]
    across += [(devices - 1, devices - 3), (devices - 3, devices - 2), (devices - 2, devices - 1)]
    for k in range(3, devices - 4, 2):
        across += [(k, k + 1), (k + 1, k)]
    steps = [1 << k for k in range(1, devices.bit_length() - 1)]
    order = [(6, 3, 5)] + [(distance + 1,) for distance in steps[2:]]
    for place, masks in enumerate(order):
        if place == 0:
            total, outer = lax.optimization_barrier((total, outer))
            outer = lax.ppermute(outer, AXES, across)
        if place == 1:
            total, fir_taps, space_taps = lax.optimization_barrier((total, fir_taps, space_taps))
            tables = pl.pallas_call(
                tables_kernel,
                out_shape=[
                    jax.ShapeDtypeStruct((channels, 6 * (channels + 2 * HALO)), BF16),
                    jax.ShapeDtypeStruct((6 * LANES, 2 * LANES), BF16),
                    jax.ShapeDtypeStruct((2 * LANES, 3 * LANES), BF16),
                ],
                in_specs=[HBM] * 2,
                out_specs=[VMEM] * 3,
                scratch_shapes=[
                    pltpu.SMEM(fir_taps.shape, F32),
                    pltpu.SMEM(space_taps.shape, F32),
                    pltpu.SemaphoreType.DMA((2,)),
                ],
                compiler_params=SMALL,
                name="tables",
            )(in_hbm(fir_taps), in_hbm(space_taps))
        if place == len(order) - 1:
            total, *tables = lax.optimization_barrier((total, *tables))
            shifted = pl.pallas_call(
                channels_kernel,
                out_shape=jax.ShapeDtypeStruct(
                    (LAGS // STEP * channels, samples + LANES), BF16
                ),
                in_specs=[VMEM] * 6,
                out_specs=VMEM,
                compiler_params=SMALL,
                name="channels",
            )(near, beside, outer, *tables)
        received = [partner(total, mask) for mask in masks]
        if place < len(order) - 1:
            total = sum(received, total)
    received, shifted = lax.optimization_barrier((received, shifted))
    mine = pl.pallas_call(
        norm_kernel,
        out_shape=jax.ShapeDtypeStruct((16, samples // 2), BF16),
        in_specs=[VMEM] * (3 + len(received)),
        out_specs=VMEM,
        compiler_params=SMALL,
        name="norm",
    )(total, *received, *tables[1:])
    other = partner(mine, 1)
    sums = jax.ShapeDtypeStruct((HALF_ROWS, channels, LAGS), F32)
    groups = -(-HALF_ROWS * STEP // LANES)
    first = pl.pallas_call(
        first_kernel,
        out_shape=sums,
        in_specs=[VMEM] * 2,
        out_specs=VMEM,
        compiler_params=SMALL,
        name="first",
    )(mine, shifted)
    out = pl.pallas_call(
        second_kernel,
        out_shape=jax.ShapeDtypeStruct((ROWS, channels, LAGS), F32),
        in_specs=[VMEM] * 3,
        out_specs=HBM,
        scratch_shapes=[pltpu.VMEM(sums.shape, F32), pltpu.SemaphoreType.DMA((1 + groups,))],
        compiler_params=SMALL,
        name="second",
    )(other, shifted, first)
    return out.reshape(PANELS, SRC, channels, LAGS)


def solution(mesh):
    return jax.shard_map(
        local,
        mesh=mesh,
        in_specs=(P(AXES, None), P(), P(), P()),
        out_specs=P(None, None, AXES, None),
        check_vma=False,
    )
```

```python
import functools

import jax
import jax.numpy as jnp
from jax import lax
from jax.experimental import pallas as pl
from jax.experimental.pallas import tpu as pltpu
from jax.sharding import PartitionSpec as P

RUN = 64
LAGS = 256
PANELS = 3
SRC = 4
AXES = ("fibre", "seg")
LANES = 128
STEP = 32
HALO = 16
ROWS = PANELS * SRC
HALF_ROWS = ROWS // 2
VMEM = pl.BlockSpec(memory_space=pltpu.VMEM)
HBM = pl.BlockSpec(memory_space=pltpu.HBM)
SMALL = pltpu.CompilerParams(vmem_limit_bytes=16 * 2**20)
BF16 = jnp.bfloat16
F32 = jnp.float32


def split(x):
    high = x.astype(BF16)
    return high, (x - high.astype(F32)).astype(BF16)


def thirds(x):
    high = x.astype(BF16).astype(F32)
    rest = x - high
    middle = rest.astype(BF16).astype(F32)
    return high, middle, rest - middle


def data_terms(x, axis):
    high, middle, low = thirds(x)
    return jnp.concatenate([high, high, middle, high, low, middle], axis=axis).astype(BF16)


def tap_terms(x, axis):
    high, middle, low = thirds(x)
    return jnp.concatenate([high, middle, high, low, high, middle], axis=axis).astype(BF16)


def taps_at(taps_ref, index):
    total = jnp.zeros(index.shape, F32)
    for j in range(taps_ref.shape[0]):
        total = jnp.where(index == j, taps_ref[j], total)
    return total


def fir_matrix(fir_ref):
    lane = lax.broadcasted_iota(jnp.int32, (8, LANES), 1)
    row = lax.broadcasted_iota(jnp.int32, (8, LANES), 0)
    first = taps_at(fir_ref, lane - row)
    first = jnp.concatenate([first, jnp.zeros_like(first)], axis=1)
    return jnp.concatenate(
        [first if g == 0 else pltpu.roll(first, 8 * g, 1) for g in range(LANES // 8)], axis=0
    )


def to_blocks(x):
    return jnp.concatenate(
        [x[:, k : k + LANES] for k in range(0, x.shape[1], LANES)], axis=0
    )


def from_blocks(x, rows):
    return jnp.concatenate([x[k : k + rows] for k in range(0, x.shape[0], rows)], axis=1)


def earlier(x, rows):
    return jnp.concatenate([jnp.zeros((rows, x.shape[1]), x.dtype), x[:-rows]], axis=0)


def later(x, rows):
    return jnp.concatenate([x[rows:], jnp.zeros((rows, x.shape[1]), x.dtype)], axis=0)


def window_bands():
    u = lax.broadcasted_iota(jnp.int32, (2 * LANES, LANES), 0) % LANES
    t = lax.broadcasted_iota(jnp.int32, (2 * LANES, LANES), 1)
    bands = [jnp.abs(u - t) <= RUN, u - t >= LANES - RUN, t - u >= LANES - RUN]
    return jnp.concatenate([jnp.where(b, 1.0, 0.0).astype(BF16) for b in bands], axis=1)


def filter_and_norm(x, fir_terms, window):
    rows, samples = x.shape
    dot = functools.partial(jnp.dot, preferred_element_type=F32)
    full = dot(data_terms(to_blocks(x), 1), fir_terms)
    smooth = full[:, :LANES] + earlier(full[:, LANES:], rows)
    high, low = split(jnp.abs(smooth))
    sums = dot(jnp.concatenate([high, low], axis=1), window)
    total = (
        sums[:, :LANES]
        + earlier(sums[:, LANES : 2 * LANES], rows)
        + later(sums[:, 2 * LANES :], rows)
    )
    shape = total.shape
    where = lax.broadcasted_iota(jnp.int32, shape, 0) // rows * LANES
    where = where + lax.broadcasted_iota(jnp.int32, shape, 1)
    count = jnp.minimum(where, RUN) + jnp.minimum(samples - 1 - where, RUN) + 1
    scale = count.astype(F32)
    return from_blocks(smooth * scale / (total + 1e-5 * scale), rows)


def pack(x):
    width = x.shape[1] // 4
    tail = x[:, 3 * width :]
    more = [
        jnp.concatenate([tail[k : k + 1] for k in range(3 * g, 3 * g + 3)], axis=1)
        for g in range(2)
    ]
    return jnp.concatenate([x[:, : 3 * width]] + more, axis=0)


def unpack(x):
    width = x.shape[1] // 3
    tail = [x[6 + k // 3 : 7 + k // 3, k % 3 * width : (k % 3 + 1) * width] for k in range(6)]
    return jnp.concatenate([x[:6], jnp.concatenate(tail, axis=0)], axis=1)


def parity(number):
    total = 0
    for k in range(16):
        total = total ^ (number >> k)
    return total & 1


def fetch(pairs, sems):
    copies = [pltpu.make_async_copy(a, b, sems.at[i]) for i, (a, b) in enumerate(pairs)]
    for copy in copies:
        copy.start()
    return copies


def load_kernel(
    strain_hbm,
    space_hbm,
    sources_hbm,
    near_ref,
    outer_ref,
    part_ref,
    matrix_ref,
    space_ref,
    sources_ref,
    sems,
):
    copies = fetch(
        [(sources_hbm, sources_ref), (space_hbm, space_ref), (strain_hbm, near_ref)], sems
    )
    channels = near_ref.shape[0]
    me = lax.axis_index(AXES)
    half = parity(me)
    half_span = (space_ref.shape[0] - 1) // 2
    copies[0].wait()
    shape = (16, 2 * channels)
    row = lax.broadcasted_iota(jnp.int32, shape, 0)
    lane = lax.broadcasted_iota(jnp.int32, shape, 1)
    source = jnp.full(shape, -(1 << 20), jnp.int32)
    for k in range(HALF_ROWS):
        number = half * HALF_ROWS + k
        source = jnp.where(row == k, sources_ref[number // SRC, number % SRC], source)
    copies[1].wait()
    matrix = taps_at(space_ref, lane + (me - me % 2) * channels - source + half_span)
    even = me % 2 == 0
    own = jnp.where(even, matrix[:, :channels], matrix[:, channels:])
    other = jnp.where(even, matrix[:, channels:], matrix[:, :channels])
    matrix_ref[...] = tap_terms(other, 1)
    copies[2].wait()
    x = near_ref[...]
    outer_ref[...] = jnp.where(even, x[:HALO], x[channels - HALO :])
    part = jnp.dot(tap_terms(own, 1), data_terms(x, 0), preferred_element_type=F32)
    part_ref[...] = pack(part[:HALF_ROWS])


def share_kernel(other_ref, part_ref, matrix_ref, outer_ref, total_ref, sent_ref):
    del outer_ref
    me, channels = lax.axis_index(AXES), other_ref.shape[0]

    @pl.when(me == 0)
    def _():
        sent_ref[...] = other_ref[channels - HALO :, :]

    @pl.when(me == lax.axis_size(AXES) - 1)
    def _():
        sent_ref[...] = other_ref[:HALO, :]

    part = jnp.dot(matrix_ref[...], data_terms(other_ref[...], 0), preferred_element_type=F32)
    total_ref[...] = part_ref[...] + pack(part[:HALF_ROWS])


def tables_kernel(
    fir_hbm, space_hbm, space_matrix_ref, fir_matrix_ref, window_ref, fir_ref, space_ref, sems
):
    copies = fetch([(space_hbm, space_ref), (fir_hbm, fir_ref)], sems)
    window_ref[...] = window_bands()
    channels = space_matrix_ref.shape[0]
    half_span = (space_ref.shape[0] - 1) // 2
    row = lax.broadcasted_iota(jnp.int32, (channels, channels + 2 * HALO), 0)
    column = lax.broadcasted_iota(jnp.int32, (channels, channels + 2 * HALO), 1)
    copies[0].wait()
    space_matrix_ref[...] = tap_terms(
        taps_at(space_ref, column - HALO - row + half_span), 1
    )
    copies[1].wait()
    fir_matrix_ref[...] = tap_terms(fir_matrix(fir_ref), 0)


def channels_kernel(
    strain_ref,
    other_ref,
    outer_ref,
    space_matrix_ref,
    fir_matrix_ref,
    window_ref,
    shifted_ref,
):
    channels, samples = strain_ref.shape
    me = lax.axis_index(AXES)
    even = me % 2 == 0
    other, outer = other_ref[...], outer_ref[...]
    outer = jnp.where((me == 0) | (me == lax.axis_size(AXES) - 1), 0.0, outer)
    before = jnp.where(even, outer, other[channels - HALO :])
    after = jnp.where(even, other[:HALO], outer)
    x = jnp.concatenate([before, strain_ref[...], after], axis=0)
    spaced = jnp.dot(space_matrix_ref[...], data_terms(x, 0), preferred_element_type=F32)
    normed = filter_and_norm(spaced, fir_matrix_ref[...], window_ref[...])
    length = shifted_ref.shape[1]
    padded = jnp.concatenate(
        [
            jnp.zeros((channels, LANES), F32),
            normed,
            jnp.zeros((channels, 2 * LANES), F32),
        ],
        axis=1,
    )
    per_tile = LANES // STEP
    for q in range(0, per_tile, 2):
        turned = [
            padded if k == 0 else pltpu.roll(padded, padded.shape[1] - STEP * k, 1)
            for k in (q, q + 1)
        ]
        pair = jnp.concatenate(turned, axis=0).astype(BF16)
        for h in range(LAGS // LANES):
            at = (h * per_tile + q) * channels
            shifted_ref[at : at + 2 * channels, :] = pair[:, h * LANES : h * LANES + length]


def swap(upper, lower, distance, lane):
    near = (lane // distance) % 2 == 0
    return (
        jnp.where(near, upper, pltpu.roll(lower, distance, 1)),
        jnp.where(near, pltpu.roll(upper, LANES - distance, 1), lower),
    )


def lag_sums(shifted_ref, normed):
    rows = HALF_ROWS
    samples = normed.shape[1]
    coarse = LAGS // STEP
    channels = shifted_ref.shape[0] // coarse
    padded = jnp.concatenate([normed, jnp.zeros((normed.shape[0], LANES), F32)], axis=1)
    lane = lax.broadcasted_iota(jnp.int32, (STEP, LANES), 1)
    row = lax.broadcasted_iota(jnp.int32, (STEP, LANES), 0)
    straight = lane >= row
    records = []
    for k in range(rows):
        one = jnp.broadcast_to(padded[k : k + 1], (STEP, padded.shape[1]))
        tiles = [
            pltpu.roll(one[:, j : j + LANES], 0, 1, stride=1, stride_axis=0)
            for j in range(0, padded.shape[1], LANES)
        ]
        previous = [tiles[-1]] + tiles[:-1]
        records.append(
            jnp.concatenate(
                [jnp.where(straight, b, a) for a, b in zip(previous, tiles)], axis=1
            ).astype(BF16)
        )
    records = jnp.concatenate(records, axis=0)
    result = lax.dot_general(
        shifted_ref[...], records, (((1,), (1,)), ((), ())), preferred_element_type=F32
    )
    result = result * float(samples) ** -0.5
    per_tile = LANES // STEP
    tiles = -(-rows // per_tile)
    short = tiles * LANES - result.shape[1]
    if short:
        result = jnp.concatenate([result, jnp.zeros((result.shape[0], short), F32)], axis=1)
    lane = lax.broadcasted_iota(jnp.int32, (channels, LANES), 1)
    for tile in range(tiles):
        count = min(per_tile, rows - tile * per_tile)
        sums = [[] for _ in range(count)]
        for h in range(LAGS // LANES):
            parts = [
                result[
                    (h * per_tile + q) * channels : (h * per_tile + q + 1) * channels,
                    tile * LANES : (tile + 1) * LANES,
                ]
                for q in range(per_tile)
            ]
            for distance in [d for d in (8, 4, 2, 1) if d < per_tile]:
                for q in range(per_tile):
                    if q & distance == 0:
                        parts[q], parts[q + distance] = swap(
                            parts[q], parts[q + distance], distance * STEP, lane
                        )
            for q in range(count):
                sums[q].append(parts[q])
        yield tile * per_tile, [jnp.concatenate(halves, axis=1) for halves in sums]


def norm_kernel(*refs):
    *parts, fir_matrix_ref, window_ref, normed_ref = refs
    spaced = unpack(sum([ref[...] for ref in parts[1:]], parts[0][...]))
    samples = spaced.shape[1]
    spaced = jnp.concatenate([spaced, jnp.zeros((8 - HALF_ROWS, samples), F32)], axis=0)
    normed = filter_and_norm(spaced, fir_matrix_ref[...], window_ref[...])
    normed = jnp.concatenate([normed[:, : samples // 2], normed[:, samples // 2 :]], axis=0)
    normed_ref[...] = normed.astype(BF16)


def rows_of(normed_ref):
    x = normed_ref[...].astype(F32)
    return jnp.concatenate([x[:8], x[8:]], axis=1)


def first_kernel(normed_ref, shifted_ref, sums_ref):
    for start, group in lag_sums(shifted_ref, rows_of(normed_ref)):
        for k, sums in enumerate(group):
            sums_ref[start + k] = sums


def second_kernel(normed_ref, shifted_ref, sums_ref, out_hbm, more_ref, sems):
    mine = parity(lax.axis_index(AXES))
    early = pltpu.make_async_copy(
        sums_ref, out_hbm.at[pl.ds(mine * HALF_ROWS, HALF_ROWS)], sems.at[0]
    )
    early.start()
    copies = [early]
    for start, group in lag_sums(shifted_ref, rows_of(normed_ref)):
        for k, sums in enumerate(group):
            more_ref[start + k] = sums
        late = pltpu.make_async_copy(
            more_ref.at[pl.ds(start, len(group))],
            out_hbm.at[pl.ds((1 - mine) * HALF_ROWS + start, len(group))],
            sems.at[len(copies)],
        )
        late.start()
        copies.append(late)
    for copy in copies:
        copy.wait()


def in_hbm(x):
    return pltpu.with_memory_space_constraint(x, pltpu.HBM)


def local(strain, fir_taps, space_taps, sources):
    channels, samples = strain.shape
    devices = lax.axis_size(AXES)

    def partner(x, mask):
        return lax.ppermute(x, AXES, [(i, i ^ mask) for i in range(devices)])

    beside = partner(strain, 1)
    packed = jax.ShapeDtypeStruct((8, samples * 3 // 4), F32)
    near, outer, part, matrix = pl.pallas_call(
        load_kernel,
        out_shape=[
            jax.ShapeDtypeStruct(strain.shape, F32),
            jax.ShapeDtypeStruct((HALO, samples), F32),
            packed,
            jax.ShapeDtypeStruct((16, 6 * channels), BF16),
        ],
        in_specs=[HBM] * 3,
        out_specs=[VMEM] * 4,
        scratch_shapes=[
            pltpu.SMEM(space_taps.shape, F32),
            pltpu.SMEM(sources.shape, jnp.int32),
            pltpu.SemaphoreType.DMA((3,)),
        ],
        compiler_params=SMALL,
        name="load",
    )(*[in_hbm(x) for x in (strain, space_taps, sources)])
    total, outer = pl.pallas_call(
        share_kernel,
        out_shape=[packed, jax.ShapeDtypeStruct(outer.shape, F32)],
        in_specs=[VMEM] * 4,
        out_specs=[VMEM] * 2,
        input_output_aliases={3: 1},
        compiler_params=SMALL,
        name="share",
    )(beside, part, matrix, outer)
    across = [(0, 2), (2, 1), (1, 0)]
    across += [(devices - 1, devices - 3), (devices - 3, devices - 2), (devices - 2, devices - 1)]
    for k in range(3, devices - 4, 2):
        across += [(k, k + 1), (k + 1, k)]
    steps = [1 << k for k in range(1, devices.bit_length() - 1)]
    order = [(6, 3, 5)] + [(distance + 1,) for distance in steps[2:]]
    for place, masks in enumerate(order):
        if place == 0:
            total, outer = lax.optimization_barrier((total, outer))
            outer = lax.ppermute(outer, AXES, across)
        if place == 1:
            total, fir_taps, space_taps = lax.optimization_barrier((total, fir_taps, space_taps))
            tables = pl.pallas_call(
                tables_kernel,
                out_shape=[
                    jax.ShapeDtypeStruct((channels, 6 * (channels + 2 * HALO)), BF16),
                    jax.ShapeDtypeStruct((6 * LANES, 2 * LANES), BF16),
                    jax.ShapeDtypeStruct((2 * LANES, 3 * LANES), BF16),
                ],
                in_specs=[HBM] * 2,
                out_specs=[VMEM] * 3,
                scratch_shapes=[
                    pltpu.SMEM(fir_taps.shape, F32),
                    pltpu.SMEM(space_taps.shape, F32),
                    pltpu.SemaphoreType.DMA((2,)),
                ],
                compiler_params=SMALL,
                name="tables",
            )(in_hbm(fir_taps), in_hbm(space_taps))
        if place == len(order) - 1:
            total, *tables = lax.optimization_barrier((total, *tables))
            shifted = pl.pallas_call(
                channels_kernel,
                out_shape=jax.ShapeDtypeStruct(
                    (LAGS // STEP * channels, samples + LANES), BF16
                ),
                in_specs=[VMEM] * 6,
                out_specs=VMEM,
                compiler_params=SMALL,
                name="channels",
            )(near, beside, outer, *tables)
        received = [partner(total, mask) for mask in masks]
        if place < len(order) - 1:
            total = sum(received, total)
    received, shifted = lax.optimization_barrier((received, shifted))
    mine = pl.pallas_call(
        norm_kernel,
        out_shape=jax.ShapeDtypeStruct((16, samples // 2), BF16),
        in_specs=[VMEM] * (3 + len(received)),
        out_specs=VMEM,
        compiler_params=SMALL,
        name="norm",
    )(total, *received, *tables[1:])
    other = partner(mine, 1)
    sums = jax.ShapeDtypeStruct((HALF_ROWS, channels, LAGS), F32)
    groups = -(-HALF_ROWS * STEP // LANES)
    first = pl.pallas_call(
        first_kernel,
        out_shape=sums,
        in_specs=[VMEM] * 2,
        out_specs=VMEM,
        compiler_params=SMALL,
        name="first",
    )(mine, shifted)
    out = pl.pallas_call(
        second_kernel,
        out_shape=jax.ShapeDtypeStruct((ROWS, channels, LAGS), F32),
        in_specs=[VMEM] * 3,
        out_specs=HBM,
        scratch_shapes=[pltpu.VMEM(sums.shape, F32), pltpu.SemaphoreType.DMA((1 + groups,))],
        compiler_params=SMALL,
        name="second",
    )(other, shifted, first)
    return out.reshape(PANELS, SRC, channels, LAGS)


def solution(mesh):
    return jax.shard_map(
        local,
        mesh=mesh,
        in_specs=(P(AXES, None), P(), P(), P()),
        out_specs=P(None, None, AXES, None),
        check_vma=False,
    )
```
